256 devices in a mesh: lon: 32 (over z, x_lo, core), lat: 8 (over y, x_hi).
Axes of the slice: x: 4 (x_hi: 2, x_lo: 2; x = x_hi * 2 + x_lo), y: 4, z: 8, core: 2. Of those that a mesh axis runs over, the one named last changes fastest.
Arguments:
- latents: bfloat16 [4, 96, 192, 1024], P(None, 'lat', 'lon'), may hold values from -6 to 6
- qkv_weight: bfloat16 [1024, 3072], replicated, may hold values from -0.1875 to 0.1875
- proj_weight: bfloat16 [1024, 1024], replicated, may hold values from -0.1875 to 0.1875
- merge_weight: bfloat16 [4096, 2048], P('lon'), may hold values from -0.09375 to 0.09375
- bias_table: float32 [16, 759], replicated, may hold values from -4 to 310
- bias_index: int32 [144, 144], replicated, may hold values from 0 to 758
- cotangent: bfloat16 [4, 48, 96, 2048], P(None, 'lat', 'lon'), may hold values from -6 to 6
Outputs:
- merged: bfloat16 [4, 48, 96, 2048], P(None, 'lat', 'lon')
- grad_latents: bfloat16 [4, 96, 192, 1024], P(None, 'lat', 'lon')
- grad_bias: float32 [16, 759], replicated
The draws below stay inside these ranges and needn't reach their ends.
All inputs are finite; a program needn't handle non-finite values.
Results may differ from the reference program's by a relative error of at most 0.02.
Values may be sent and summed in bfloat16 or wider, within the bound.
A program may use at most 128 MiB of HBM per device.

```python
import jax
import jax.numpy as jnp
from jax import lax

D = 1024
HEADS = 16
OUT = 2048
LEVELS = 4
WIN_LEV = 2
WIN_LAT = 12
WIN_LON = 6
NLAT = 96
NLON = 192
NBIAS = 759


def draw_bias_table(key, part):
    key = jax.random.fold_in(key, 7)
    base = jnp.clip(jax.random.normal(key, (HEADS, NBIAS), jnp.float32), -4.0, 4.0)
    return base


def set_ends(result, stream_key, least, top_value):
    longest = result.shape.index(max(result.shape))
    spots = []
    for shift in (0, 1):
        where = [jax.random.randint(jax.random.fold_in(stream_key, axis), (), 0, length) for axis, length in enumerate(result.shape)]
        where[longest] = (where[longest] + shift) % result.shape[longest]
        spots.append(tuple(where))
    return result.at[spots[0]].set(least).at[spots[1]].set(top_value)


def levels(rng, dims, pieces, low, top_value):
    level, own = 1.0, jax.random.fold_in(rng, 6)
    for dim, parts in pieces:
        steps = jnp.exp(jax.random.uniform(jax.random.fold_in(own, dim), (parts,), jnp.float32, low / len(pieces), top_value / len(pieces)))
        level = level * jnp.repeat(steps, dims[dim] // parts).reshape([-1 if axis == dim else 1 for axis in range(len(dims))])
    return level


def bell_draw(stream_key, extent, scale, most, pieces=(), held_as=jnp.bfloat16):
    result = jax.random.normal(stream_key, extent, jnp.float32) * scale
    if len(pieces) > 0:
        result = levels(stream_key, extent, pieces, -0.22, 0.18) * result
    return jnp.clip(result, min=-most, max=most).astype(held_as)


def setup_inputs(seed: int = 0) -> dict:
    key_list = jax.random.split(jax.random.key(seed), 8)
    latents = bell_draw(key_list[0], (LEVELS, NLAT, NLON, D), 1.0, 6.0, ((1, 8), (2, 32)))
    qkv_weight = bell_draw(key_list[1], (D, 3 * D), D ** -0.5, 0.1875)
    proj_weight = bell_draw(key_list[2], (D, D), D ** -0.5, 0.1875)
    merge_weight = bell_draw(key_list[3], (4 * D, OUT), (4 * D) ** -0.5, 0.09375, ((0, 32),))
    bias_table = draw_bias_table(jax.random.fold_in(key_list[7], 71), 0)
    bias_index = set_ends(jax.random.randint(key_list[5], (WIN_LEV * WIN_LAT * WIN_LON, WIN_LEV * WIN_LAT * WIN_LON), 0, NBIAS), jax.random.fold_in(key_list[5], 1), 0, NBIAS - 1).astype(jnp.int32)
    cotangent = bell_draw(key_list[6], (LEVELS, NLAT // 2, NLON // 2, OUT), 1.0, 6.0, ((1, 8), (2, 32)))
    return {"latents": latents, "qkv_weight": qkv_weight, "proj_weight": proj_weight, "merge_weight": merge_weight, "bias_table": bias_table, "bias_index": bias_index, "cotangent": cotangent}


EPS = 1e-05
MASKED = -1e+30

def normalize(values):
    average = lax.optimization_barrier(jnp.mean(values, axis=-1, keepdims=True))
    centered = values - average
    variance = lax.optimization_barrier(jnp.mean(centered * centered, axis=-1, keepdims=True))
    return centered * lax.rsqrt(variance + EPS)

def to_windows(grid_cells):
    level_count, lat_rows, lon_cols, features = grid_cells.shape
    shaped = grid_cells.reshape(level_count // WIN_LEV, WIN_LEV, lat_rows // WIN_LAT, WIN_LAT, lon_cols // WIN_LON, WIN_LON, features)
    shaped = shaped.transpose(0, 2, 4, 1, 3, 5, 6)
    return shaped.reshape(-1, WIN_LEV * WIN_LAT * WIN_LON, features)

def from_windows(window_rows, level_count, lat_rows, lon_cols):
    features = window_rows.shape[-1]
    shaped = window_rows.reshape(level_count // WIN_LEV, lat_rows // WIN_LAT, lon_cols // WIN_LON, WIN_LEV, WIN_LAT, WIN_LON, features)
    shaped = shaped.transpose(0, 3, 1, 4, 2, 5, 6)
    return shaped.reshape(level_count, lat_rows, lon_cols, features)

def lat_regions(row_ids, total_rows):
    return jnp.where(row_ids < total_rows - WIN_LAT, 0, jnp.where(row_ids < total_rows - WIN_LAT // 2, 1, 2)).astype(jnp.int32)

def region_labels(lat_ids, level_count, lon_cols):
    level_ids = jnp.arange(level_count, dtype=jnp.int32)
    region_ids = jnp.where(level_ids < level_count - WIN_LEV, 0, jnp.where(level_ids < level_count - WIN_LEV // 2, 1, 2)).astype(jnp.int32)
    labels = lat_ids[None, :, None] * 3 + region_ids[:, None, None]
    return jnp.broadcast_to(labels, (level_count, lat_ids.shape[0], lon_cols)).astype(jnp.int32)

def attend(window_rows, window_labels, bias_table, bias_index, qkv_weight, proj_weight):
    num_windows, window_size, features = window_rows.shape
    head_count = bias_table.shape[0]
    head_dim = features // head_count
    flat_rows = window_rows.reshape(num_windows * window_size, features)
    normed = normalize(flat_rows.astype(jnp.float32)).astype(jnp.bfloat16)
    packed = jnp.dot(normed, qkv_weight, preferred_element_type=jnp.float32).astype(jnp.bfloat16)
    packed = packed.reshape(num_windows, window_size, 3, head_count, head_dim).astype(jnp.float32)
    scores = jnp.einsum('wqhd,wkhd->whqk', packed[:, :, 0], packed[:, :, 1]) * head_dim ** (-0.5)
    bias_terms = jnp.take(bias_table, bias_index, axis=1)
    allowed = window_labels[:, None, :, None] == window_labels[:, None, None, :]
    scores = jnp.where(allowed, scores + bias_terms[None], MASKED)
    row_max = lax.optimization_barrier(jnp.max(scores, axis=-1, keepdims=True))
    weights = jnp.exp(scores - row_max)
    probabilities = (weights / lax.optimization_barrier(jnp.sum(weights, axis=-1, keepdims=True))).astype(jnp.bfloat16)
    mixed_rows = jnp.einsum('whqk,wkhd->wqhd', probabilities.astype(jnp.float32), packed[:, :, 2]).astype(jnp.bfloat16)
    mixed_rows = mixed_rows.reshape(num_windows * window_size, features)
    block_out = flat_rows.astype(jnp.float32) + jnp.dot(mixed_rows, proj_weight, preferred_element_type=jnp.float32)
    return block_out.astype(jnp.bfloat16).reshape(num_windows, window_size, features)

def merge_inputs(grid_cells):
    level_count, lat_rows, lon_cols, features = grid_cells.shape
    shaped = grid_cells.reshape(level_count, lat_rows // 2, 2, lon_cols // 2, 2, features)
    shaped = shaped.transpose(0, 1, 3, 4, 2, 5)
    shaped = shaped.reshape(level_count * (lat_rows // 2) * (lon_cols // 2), 4 * features)
    return normalize(shaped.astype(jnp.float32)).astype(jnp.bfloat16)

def encode(tokens, bias_table, qkv_weight, proj_weight, merge_weight, bias_index):
    level_count, lat_rows, lon_cols, features = tokens.shape
    shifts = (WIN_LEV // 2, WIN_LAT // 2, WIN_LON // 2)
    rolled = jnp.roll(tokens, (-shifts[0], -shifts[1], -shifts[2]), axis=(0, 1, 2))
    lat_ids = lat_regions(jnp.arange(lat_rows, dtype=jnp.int32), lat_rows)
    labels = region_labels(lat_ids, level_count, lon_cols)
    window_rows = to_windows(rolled)
    window_labels = to_windows(labels[..., None])[..., 0]
    window_size = WIN_LEV * WIN_LAT * WIN_LON
    per_group = lon_cols // WIN_LON

    def attend_group(packed_pair):
        return attend(packed_pair[0], packed_pair[1], bias_table, bias_index, qkv_weight, proj_weight)
    grouped = lax.map(attend_group, (window_rows.reshape(-1, per_group, window_size, features), window_labels.reshape(-1, per_group, window_size)))
    block_grid = from_windows(grouped.reshape(-1, window_size, features), level_count, lat_rows, lon_cols)
    restored = jnp.roll(block_grid, shifts, axis=(0, 1, 2))
    merge_in = merge_inputs(restored)
    merged = jnp.dot(merge_in, merge_weight, preferred_element_type=jnp.float32).astype(jnp.bfloat16)
    return merged.reshape(level_count, lat_rows // 2, lon_cols // 2, merge_weight.shape[1])

def reference(latents, qkv_weight, proj_weight, merge_weight, bias_table, bias_index, cotangent):

    def forward_pass(tokens, table_values):
        return encode(tokens, table_values, qkv_weight, proj_weight, merge_weight, bias_index)
    merged, pullback = jax.vjp(forward_pass, latents, bias_table)
    grad_latents, grad_bias = pullback(cotangent)
    return (merged, grad_latents, grad_bias)
```

```python
import jax
import jax.numpy as jnp
from jax import lax
from jax.experimental import pallas as pl
from jax.experimental.pallas import tpu as pltpu
from jax.sharding import PartitionSpec as P

EPS = 1e-05
MASKED = -1e30
HEADS = 16
PAIRS = 8
HEAD_DIM = 64
WINDOW = 144
WINDOWS = 2
TOKENS = WINDOW * WINDOWS
WIDTH = 1024
BUCKETS = 768
LANES = 128
SPLIT = 256
WIN_LEV = 2
WIN_LAT = 12
WIN_LON = 6
F32 = jnp.float32
BF16 = jnp.bfloat16
LAST = (((1,), (1,)), ((), ()))
FIRST = (((0,), (0,)), ((), ()))


def dot(a, b, dims=(((1,), (0,)), ((), ()))):
    return lax.dot_general(a, b, dims, preferred_element_type=F32)


def stats(values):
    average = jnp.mean(values, axis=-1, keepdims=True)
    centered = values - average
    variance = jnp.mean(centered * centered, axis=-1, keepdims=True)
    return centered, lax.rsqrt(variance + EPS)


def half_mask(shape, half):
    lane = lax.broadcasted_iota(jnp.int32, shape, 1)
    return (lane >= HEAD_DIM) if half else (lane < HEAD_DIM)


def region_code(shape, axis, window, is_last):
    token = lax.broadcasted_iota(jnp.int32, shape, axis)
    level = (token >= 72).astype(jnp.int32)
    row = token - 72 * level
    late = (row >= 36).astype(jnp.int32)
    return late * is_last + (2 * level if window == 1 else 0)


def allowed_pairs(window, is_last):
    shape = (WINDOW, WINDOW)
    return region_code(shape, 0, window, is_last) == region_code(shape, 1, window, is_last)


def gather_bias(table_ref, index_ref, head):
    tiles = []
    for tile in range(2):
        index = index_ref[:, tile * LANES:(tile + 1) * LANES]
        low = index & (LANES - 1)
        high = index >> 7
        found = None
        for chunk in range(BUCKETS // LANES):
            row = table_ref[head:head + 1, chunk * LANES:(chunk + 1) * LANES]
            spread = jnp.broadcast_to(row, (WINDOW, LANES))
            part = jnp.take_along_axis(spread, low, axis=1, mode="promise_in_bounds")
            found = part if found is None else jnp.where(high == chunk, part, found)
        tiles.append(found)
    return jnp.concatenate(tiles, axis=1)[:, :WINDOW]


def forward_body(is_last, x_ref, table_ref, index_ref, wqkv_ref, wproj_ref, out_ref, packed_ref, probs_ref, normed, attended):
    centered, inverse = stats(x_ref[...].astype(F32))
    normed[...] = (centered * inverse).astype(BF16)
    for part in range(12):
        cols = slice(part * 256, (part + 1) * 256)
        packed_ref[:, cols] = dot(normed[...], wqkv_ref[:, cols]).astype(BF16)
    allowed = [allowed_pairs(window, is_last) for window in range(WINDOWS)]
    for pair in range(PAIRS):
        bias = [gather_bias(table_ref, index_ref, 2 * pair + half) for half in range(2)]
        for window in range(WINDOWS):
            rows = slice(window * WINDOW, (window + 1) * WINDOW)
            base = pair * LANES
            query = packed_ref[rows, base:base + LANES] * jnp.array(HEAD_DIM ** -0.5, BF16)
            key = packed_ref[rows, WIDTH + base:WIDTH + base + LANES]
            value = packed_ref[rows, 2 * WIDTH + base:2 * WIDTH + base + LANES]
            masks = [half_mask((WINDOW, LANES), half) for half in range(2)]
            zero = jnp.zeros((WINDOW, LANES), BF16)
            mixed = None
            for half in range(2):
                scores = dot(jnp.where(masks[half], query, zero), key, LAST)
                scores = jnp.where(allowed[window], scores + bias[half], MASKED)
                weights = jnp.exp(scores - jnp.max(scores, axis=-1, keepdims=True))
                probs = (weights * (1.0 / jnp.sum(weights, axis=-1, keepdims=True))).astype(BF16)
                probs_ref[window, 2 * pair + half] = probs
                term = dot(probs, jnp.where(masks[half], value, zero))
                mixed = term if mixed is None else mixed + term
            attended[rows, base:base + LANES] = mixed.astype(BF16)
    for part in range(4):
        cols = slice(part * 256, (part + 1) * 256)
        out_ref[:, cols] = (x_ref[:, cols].astype(F32) + dot(attended[...], wproj_ref[:, cols])).astype(BF16)


def forward_kernel(x_ref, table_ref, index_ref, wqkv_ref, wproj_ref, out_ref, packed_ref, probs_ref, normed, attended):
    is_last = (lax.axis_index("lat") == lax.axis_size("lat") - 1).astype(jnp.int32)
    forward_body(is_last, x_ref, table_ref, index_ref, wqkv_ref, wproj_ref, out_ref, packed_ref, probs_ref, normed, attended)


def forward_call(x, table, index, wqkv, wproj, kernel=forward_kernel):
    return pl.pallas_call(
        kernel,
        out_shape=(
            jax.ShapeDtypeStruct((TOKENS, WIDTH), BF16),
            jax.ShapeDtypeStruct((TOKENS, 3 * WIDTH), BF16),
            jax.ShapeDtypeStruct((WINDOWS, HEADS, WINDOW, WINDOW), BF16),
        ),
        in_specs=[pl.BlockSpec(memory_space=pltpu.VMEM)] * 5,
        out_specs=[pl.BlockSpec(memory_space=pltpu.VMEM)] * 3,
        scratch_shapes=[pltpu.VMEM((TOKENS, WIDTH), BF16), pltpu.VMEM((TOKENS, WIDTH), BF16)],
        compiler_params=pltpu.CompilerParams(vmem_limit_bytes=56 * 2**20),
        cost_estimate=pl.CostEstimate(flops=2 * 1400 * 2**20, bytes_accessed=16 * 2**20, transcendentals=0),
        name="attention_forward",
    )(x, table, index, wqkv, wproj)


def backward_kernel(grad_ref, x_ref, packed_ref, probs_ref, index_ref, wqkv_ref, wproj_ref, dx_ref, table_ref, datt, dpacked, dmain, dtail):
    datt[...] = dot(grad_ref[...], wproj_ref[...], LAST).astype(BF16)
    for pair in range(PAIRS):
        sums = [None, None]
        for window in range(WINDOWS):
            rows = slice(window * WINDOW, (window + 1) * WINDOW)
            base = pair * LANES
            scale = jnp.array(HEAD_DIM ** -0.5, BF16)
            query = packed_ref[rows, base:base + LANES] * scale
            key = packed_ref[rows, WIDTH + base:WIDTH + base + LANES] * scale
            value = packed_ref[rows, 2 * WIDTH + base:2 * WIDTH + base + LANES]
            out_grad = datt[rows, base:base + LANES]
            masks = [half_mask((WINDOW, LANES), half) for half in range(2)]
            zero = jnp.zeros((WINDOW, LANES), BF16)
            dquery, dkey, dvalue = None, None, None
            for half in range(2):
                grad = jnp.where(masks[half], out_grad, zero)
                probs = probs_ref[window, 2 * pair + half]
                wide = probs.astype(F32)
                dprobs = dot(grad, value, LAST)
                product = wide * dprobs
                ds = product - wide * jnp.sum(product, axis=-1, keepdims=True)
                sums[half] = ds if sums[half] is None else sums[half] + ds
                narrow = ds.astype(BF16)
                one = dot(narrow, jnp.where(masks[half], key, zero))
                two = dot(narrow, jnp.where(masks[half], query, zero), FIRST)
                three = dot(probs, grad, FIRST)
                dquery = one if dquery is None else dquery + one
                dkey = two if dkey is None else dkey + two
                dvalue = three if dvalue is None else dvalue + three
            dpacked[rows, base:base + LANES] = dquery.astype(BF16)
            dpacked[rows, WIDTH + base:WIDTH + base + LANES] = dkey.astype(BF16)
            dpacked[rows, 2 * WIDTH + base:2 * WIDTH + base + LANES] = dvalue.astype(BF16)
        for half in range(2):
            total = jnp.concatenate([sums[half], jnp.zeros((WINDOW, 2 * LANES - WINDOW), F32)], axis=1)
            for tile in range(2):
                cols = slice(tile * LANES, (tile + 1) * LANES)
                dscores = (dmain, dtail)[tile]
                dscores[pl.ds(2 * pair + half, WINDOW, stride=HEADS), :] = total[:, cols]
    dnormed = dot(dpacked[...], wqkv_ref[...], LAST).astype(BF16).astype(F32)
    centered, inverse = stats(x_ref[...].astype(F32))
    hat = centered * inverse
    slope = jnp.mean(dnormed * hat, axis=-1, keepdims=True)
    inner = inverse * (dnormed - jnp.mean(dnormed, axis=-1, keepdims=True) - hat * slope)
    dx_ref[...] = (grad_ref[...].astype(F32) + inner).astype(BF16)

    def scatter_row(row, total):
        here = pl.ds(pl.multiple_of(row * HEADS, HEADS), HEADS)
        block = jnp.concatenate([dmain[here, :], dtail[here, :]], axis=1)
        index = index_ref[pl.ds(row, 1), :]
        low = index & (SPLIT - 1)
        high = index >> 8
        parts = jnp.concatenate(
            [jnp.where(high == part, block, 0.0) for part in range(BUCKETS // SPLIT)], axis=0
        )
        coarse = parts.astype(BF16)
        fine = (parts - coarse.astype(F32)).astype(BF16)
        bucket = lax.broadcasted_iota(jnp.int32, (SPLIT, 2 * LANES), 0)
        hot = jnp.where(bucket == low, 1.0, 0.0).astype(BF16)
        return total + dot(jnp.concatenate([coarse, fine], axis=0), hot, LAST)

    rows = HEADS * (BUCKETS // SPLIT)
    total = lax.fori_loop(0, WINDOW, scatter_row, jnp.zeros((2 * rows, SPLIT), F32), unroll=4)
    total = total[:rows] + total[rows:]
    for part in range(BUCKETS // SPLIT):
        table_ref[:, part * SPLIT:(part + 1) * SPLIT] = total[part * HEADS:(part + 1) * HEADS]


def backward_call(grad, x, packed, probs, index, wqkv, wproj):
    return pl.pallas_call(
        backward_kernel,
        out_shape=(
            jax.ShapeDtypeStruct((TOKENS, WIDTH), BF16),
            jax.ShapeDtypeStruct((HEADS, BUCKETS), F32),
        ),
        in_specs=[pl.BlockSpec(memory_space=pltpu.VMEM)] * 7,
        out_specs=[pl.BlockSpec(memory_space=pltpu.VMEM)] * 2,
        scratch_shapes=[
            pltpu.VMEM((TOKENS, WIDTH), BF16),
            pltpu.VMEM((TOKENS, 3 * WIDTH), BF16),
            pltpu.VMEM((WINDOW * HEADS, LANES), F32),
            pltpu.VMEM((WINDOW * HEADS, LANES), F32),
        ],
        compiler_params=pltpu.CompilerParams(vmem_limit_bytes=56 * 2**20),
        cost_estimate=pl.CostEstimate(flops=2 * 1700 * 2**20, bytes_accessed=16 * 2**20, transcendentals=0),
        name="attention_backward",
    )(grad, x, packed, probs, index, wqkv, wproj)


def from_behind(shard, axis, by):
    devices = lax.axis_size(axis)
    return lax.ppermute(shard, axis, [(i, (i + by) % devices) for i in range(devices)])


def normalize(values):
    average = jnp.mean(values, axis=-1, keepdims=True)
    centered = values - average
    variance = jnp.mean(centered * centered, axis=-1, keepdims=True)
    return centered * lax.rsqrt(variance + EPS)


def to_windows(grid_cells):
    level_count, lat_rows, lon_cols, features = grid_cells.shape
    shaped = grid_cells.reshape(
        level_count // WIN_LEV,
        WIN_LEV,
        lat_rows // WIN_LAT,
        WIN_LAT,
        lon_cols // WIN_LON,
        WIN_LON,
        features,
    )
    shaped = shaped.transpose(0, 2, 4, 1, 3, 5, 6)
    return shaped.reshape(-1, WIN_LEV * WIN_LAT * WIN_LON, features)


def from_windows(window_rows, level_count, lat_rows, lon_cols):
    features = window_rows.shape[-1]
    shaped = window_rows.reshape(
        level_count // WIN_LEV,
        lat_rows // WIN_LAT,
        lon_cols // WIN_LON,
        WIN_LEV,
        WIN_LAT,
        WIN_LON,
        features,
    )
    shaped = shaped.transpose(0, 3, 1, 4, 2, 5, 6)
    return shaped.reshape(level_count, lat_rows, lon_cols, features)


def merge_inputs(grid_cells):
    level_count, lat_rows, lon_cols, features = grid_cells.shape
    shaped = grid_cells.reshape(level_count, lat_rows // 2, 2, lon_cols // 2, 2, features)
    shaped = shaped.transpose(0, 1, 3, 4, 2, 5)
    shaped = shaped.reshape(level_count * (lat_rows // 2) * (lon_cols // 2), 4 * features)
    return normalize(shaped.astype(jnp.float32)).astype(jnp.bfloat16)


def roll_forward(grid_cells):
    lat_shift = WIN_LAT // 2
    lon_shift = WIN_LON // 2
    grid_cells = jnp.roll(grid_cells, -(WIN_LEV // 2), axis=0)
    incoming = from_behind(grid_cells[:, :lat_shift], "lat", -1)
    grid_cells = jnp.concatenate([grid_cells[:, lat_shift:], incoming], axis=1)
    incoming = from_behind(grid_cells[:, :, :lon_shift], "lon", -1)
    return jnp.concatenate([grid_cells[:, :, lon_shift:], incoming], axis=2)


def roll_back(grid_cells):
    lat_shift = WIN_LAT // 2
    lon_shift = WIN_LON // 2
    lat_rows = grid_cells.shape[1]
    lon_cols = grid_cells.shape[2]
    incoming = from_behind(grid_cells[:, :, lon_cols - lon_shift :], "lon", 1)
    grid_cells = jnp.concatenate([incoming, grid_cells[:, :, : lon_cols - lon_shift]], axis=2)
    incoming = from_behind(grid_cells[:, lat_rows - lat_shift :], "lat", 1)
    grid_cells = jnp.concatenate([incoming, grid_cells[:, : lat_rows - lat_shift]], axis=1)
    return jnp.roll(grid_cells, WIN_LEV // 2, axis=0)


def shards(latents, qkv_weight, proj_weight, merge_weight, bias_table, bias_index, cotangent):
    level_count, lat_rows, lon_cols, features = latents.shape
    out_width = cotangent.shape[-1]
    table = jnp.pad(bias_table, ((0, 0), (0, BUCKETS - bias_table.shape[1])))
    index = jnp.pad(bias_index, ((0, 0), (0, 2 * LANES - WINDOW)))
    tokens = to_windows(roll_forward(latents)).reshape(TOKENS, WIDTH)
    block_out, packed, probs = forward_call(tokens, table, index, qkv_weight, proj_weight)
    rolled_out = from_windows(
        block_out.reshape(WINDOWS, WINDOW, WIDTH), level_count, lat_rows, lon_cols
    )
    restored = roll_back(rolled_out)
    merge_in, norm_pull = jax.vjp(merge_inputs, restored)
    token_rows = merge_in.shape[0]
    cotangent_rows = cotangent.reshape(token_rows, out_width)
    weight = lax.all_gather(merge_weight, "lon", axis=0, tiled=True)
    merged_rows = dot(merge_in, weight).astype(BF16)
    merge_grad = dot(cotangent_rows, weight, LAST).astype(BF16)
    merged = merged_rows.reshape(level_count, lat_rows // 2, lon_cols // 2, out_width)
    restored_grad = norm_pull(merge_grad)[0]
    rolled_grad = to_windows(roll_forward(restored_grad)).reshape(TOKENS, WIDTH)
    grad_rolled, grad_table = backward_call(
        rolled_grad, tokens, packed, probs, index, qkv_weight, proj_weight
    )
    grad_latents = roll_back(
        from_windows(grad_rolled.reshape(WINDOWS, WINDOW, WIDTH), level_count, lat_rows, lon_cols)
    )
    grad_bias = lax.psum(grad_table[:, :bias_table.shape[1]], ("lon", "lat"))
    return (merged, grad_latents, grad_bias)


def solution(mesh):
    return jax.shard_map(
        shards,
        mesh=mesh,
        in_specs=(
            P(None, "lat", "lon", None),
            P(),
            P(),
            P("lon", None),
            P(),
            P(),
            P(None, "lat", "lon", None),
        ),
        out_specs=(P(None, "lat", "lon", None), P(None, "lat", "lon", None), P()),
        check_vma=False,
    )
```

```python
import jax
import jax.numpy as jnp
import numpy as np
from jax import lax
from jax.experimental import pallas as pl
from jax.experimental.pallas import tpu as pltpu
from jax.sharding import PartitionSpec as P

EPS = 1e-05
MASKED = -1e30
HEADS = 16
PAIRS = 8
HEAD_DIM = 64
WINDOW = 144
WINDOWS = 2
TOKENS = WINDOW * WINDOWS
WIDTH = 1024
OUT = 2048
BUCKETS = 768
LANES = 128
SPLIT = 256
TEAM = 4
RING = 8
BANDS = 8
PIECE = 128
CELLS = 72
SLAB = 80
F32 = jnp.float32
BF16 = jnp.bfloat16
LAST = (((1,), (1,)), ((), ()))
FIRST = (((0,), (0,)), ((), ()))
MESH = pl.DeviceIdType.MESH


def dot(a, b, dims=(((1,), (0,)), ((), ()))):
    return lax.dot_general(a, b, dims, preferred_element_type=F32)


def quad_row(level, row, col):
    quad = 2 * (row // 6) + col // 3
    return quad * SLAB + level * 18 + (row % 6) * 3 + col % 3


def orders():
    natural = np.zeros((4 * SLAB, TOKENS), np.float32)
    window = np.zeros((TOKENS, 4 * SLAB), np.float32)
    merge = np.zeros((TOKENS, 4 * SLAB), np.float32)
    for level in range(4):
        for row in range(12):
            for col in range(6):
                cell = (level * 12 + row) * 6 + col
                place = quad_row(level, row, col)
                natural[place, cell] = 1
                source = quad_row((level + 1) % 4, (row + 6) % 12, (col + 3) % 6)
                window[cell, source] = 1
                spot = 2 * (col % 2) + row % 2
                merge[spot * CELLS + (level * 6 + row // 2) * 3 + col // 2, place] = 1
    return [jnp.asarray(m, BF16) for m in (natural, window, window.T, merge, merge.T, natural.T)]


def stats(values):
    average = jnp.mean(values, axis=-1, keepdims=True)
    centered = values - average
    variance = jnp.mean(centered * centered, axis=-1, keepdims=True)
    return centered, lax.rsqrt(variance + EPS)


def half_mask(shape, half):
    lane = lax.broadcasted_iota(jnp.int32, shape, 1)
    return (lane >= HEAD_DIM) if half else (lane < HEAD_DIM)


def region_code(shape, axis, window, is_last):
    token = lax.broadcasted_iota(jnp.int32, shape, axis)
    level = (token >= 72).astype(jnp.int32)
    row = token - 72 * level
    late = (row >= 36).astype(jnp.int32)
    return late * is_last + (2 * level if window == 1 else 0)


def allowed_pairs(window, is_last):
    shape = (WINDOW, WINDOW)
    return region_code(shape, 0, window, is_last) == region_code(shape, 1, window, is_last)


def gather_bias(table_ref, index_ref, head):
    tiles = []
    for tile in range(2):
        index = index_ref[:, tile * LANES:(tile + 1) * LANES]
        low = index & (LANES - 1)
        high = index >> 7
        found = None
        for chunk in range(BUCKETS // LANES):
            row = table_ref[pl.ds(head, 1), chunk * LANES:(chunk + 1) * LANES]
            spread = jnp.broadcast_to(row, (WINDOW, LANES))
            part = jnp.take_along_axis(spread, low, axis=1, mode="promise_in_bounds")
            found = part if found is None else jnp.where(high == chunk, part, found)
        tiles.append(found)
    return jnp.concatenate(tiles, axis=1)[:, :WINDOW]


def attend_pair(pair, is_last, table_ref, index_ref, packed, probs_ref, attended):
    base = pl.multiple_of(pair * LANES, LANES)
    bias = [gather_bias(table_ref, index_ref, 2 * pair + half) for half in range(2)]
    masks = [half_mask((WINDOW, LANES), half) for half in range(2)]
    zero = jnp.zeros((WINDOW, LANES), BF16)
    for window in range(WINDOWS):
        rows = slice(window * WINDOW, (window + 1) * WINDOW)
        allowed = allowed_pairs(window, is_last)
        query = packed[rows, pl.ds(base, LANES)] * jnp.array(HEAD_DIM ** -0.5, BF16)
        key = packed[rows, pl.ds(WIDTH + base, LANES)]
        value = packed[rows, pl.ds(2 * WIDTH + base, LANES)]
        mixed = None
        for half in range(2):
            scores = dot(jnp.where(masks[half], query, zero), key, LAST)
            scores = jnp.where(allowed, scores + bias[half], MASKED)
            weights = jnp.exp(scores - jnp.max(scores, axis=-1, keepdims=True))
            probs = (weights * (1.0 / jnp.sum(weights, axis=-1, keepdims=True))).astype(BF16)
            probs_ref[window, 2 * pair + half] = probs
            term = dot(probs, jnp.where(masks[half], value, zero))
            mixed = term if mixed is None else mixed + term
        attended[rows, pl.ds(base, LANES)] = mixed.astype(BF16)


def unattend_pair(pair, packed, probs_ref, datt, dpacked, dmain, dtail):
    base = pl.multiple_of(pair * LANES, LANES)
    scale = jnp.array(HEAD_DIM ** -0.5, BF16)
    masks = [half_mask((WINDOW, LANES), half) for half in range(2)]
    zero = jnp.zeros((WINDOW, LANES), BF16)
    sums = [None, None]
    for window in range(WINDOWS):
        rows = slice(window * WINDOW, (window + 1) * WINDOW)
        query = packed[rows, pl.ds(base, LANES)] * scale
        key = packed[rows, pl.ds(WIDTH + base, LANES)] * scale
        value = packed[rows, pl.ds(2 * WIDTH + base, LANES)]
        out_grad = datt[rows, pl.ds(base, LANES)]
        dquery, dkey, dvalue = None, None, None
        for half in range(2):
            grad = jnp.where(masks[half], out_grad, zero)
            probs = probs_ref[window, 2 * pair + half]
            wide = probs.astype(F32)
            product = wide * dot(grad, value, LAST)
            ds = product - wide * jnp.sum(product, axis=-1, keepdims=True)
            sums[half] = ds if sums[half] is None else sums[half] + ds
            narrow = ds.astype(BF16)
            one = dot(narrow, jnp.where(masks[half], key, zero))
            two = dot(narrow, jnp.where(masks[half], query, zero), FIRST)
            three = dot(probs, grad, FIRST)
            dquery = one if dquery is None else dquery + one
            dkey = two if dkey is None else dkey + two
            dvalue = three if dvalue is None else dvalue + three
        dpacked[rows, pl.ds(base, LANES)] = dquery.astype(BF16)
        dpacked[rows, pl.ds(WIDTH + base, LANES)] = dkey.astype(BF16)
        dpacked[rows, pl.ds(2 * WIDTH + base, LANES)] = dvalue.astype(BF16)
    for half in range(2):
        total = jnp.concatenate([sums[half], jnp.zeros((WINDOW, 2 * LANES - WINDOW), F32)], axis=1)
        for tile, store in enumerate((dmain, dtail)):
            cols = slice(tile * LANES, (tile + 1) * LANES)
            store[pl.ds(2 * pair + half, WINDOW, stride=HEADS), :] = total[:, cols]


def scatter_table(index_ref, dmain, dtail):
    def scatter_row(row, total):
        here = pl.ds(pl.multiple_of(row * HEADS, HEADS), HEADS)
        block = jnp.concatenate([dmain[here, :], dtail[here, :]], axis=1)
        index = index_ref[pl.ds(row, 1), :]
        low = index & (SPLIT - 1)
        high = index >> 8
        parts = jnp.concatenate(
            [jnp.where(high == part, block, 0.0) for part in range(BUCKETS // SPLIT)], axis=0
        )
        coarse = parts.astype(BF16)
        fine = (parts - coarse.astype(F32)).astype(BF16)
        bucket = lax.broadcasted_iota(jnp.int32, (SPLIT, 2 * LANES), 0)
        hot = jnp.where(bucket == low, 1.0, 0.0).astype(BF16)
        return total + dot(jnp.concatenate([coarse, fine], axis=0), hot, LAST)

    rows = HEADS * (BUCKETS // SPLIT)
    total = lax.fori_loop(0, WINDOW, scatter_row, jnp.zeros((2 * rows, SPLIT), F32), unroll=4)
    total = total[:rows] + total[rows:]
    return jnp.concatenate([total[part * HEADS:(part + 1) * HEADS] for part in range(BUCKETS // SPLIT)], axis=1)


def pad_rows(values):
    return jnp.concatenate([values, jnp.zeros((SLAB - CELLS, values.shape[1]), F32)], axis=0).astype(BF16)


def kernel(
    nat2quad, quad2win, win2quad, quad2merge, merge2quad, quad2nat,
    x_ref, table_ref, index_ref, cot_hbm, piece_hbm, wqkv_hbm, wproj_hbm,
    merged_ref, grad_ref, bias_ref,
    wqkv, wproj, wbuf, cots, sent, landed, tokens, normed, packed, probs, attended,
    hats, gsend, grecv, msend, mrecv, psend, precv, datt, dpacked, dmain, dtail,
    sum_team, sum_ring, sum_bands, local_sems, send_sems, recv_sems,
):
    lon = lax.axis_index("lon")
    lat = lax.axis_index("lat")
    ring = lon // TEAM
    member = lax.rem(lon, TEAM)
    lons = RING * TEAM
    is_last = (lat == BANDS - 1).astype(jnp.int32)

    def team_peer(step):
        return {"lon": ring * TEAM + lax.rem(member + step, TEAM), "lat": lat}

    def ring_peer(step):
        return {"lon": lax.rem(ring + step, RING) * TEAM + member, "lat": lat}

    def band_peer(step):
        return {"lon": lon, "lat": lax.rem(lat + step, BANDS)}

    def near(rows, cols):
        return {"lon": lax.rem(lon + cols + lons, lons), "lat": lax.rem(lat + rows + BANDS, BANDS)}

    peers = [team_peer(step) for step in range(1, TEAM)]
    peers += [ring_peer(step) for step in range(1, RING)]
    peers += [band_peer(step) for step in range(1, BANDS)]
    peers += [near(0, 1), near(0, -1), near(1, 1), near(-1, -1)]

    loads = [
        pltpu.make_async_copy(wqkv_hbm, wqkv, local_sems.at[0]),
        pltpu.make_async_copy(wproj_hbm, wproj, local_sems.at[1]),
        pltpu.make_async_copy(cot_hbm, cots.at[member], local_sems.at[2]),
        pltpu.make_async_copy(piece_hbm, wbuf.at[ring], local_sems.at[3]),
    ]
    for load in loads:
        load.start()

    barrier = pltpu.get_barrier_semaphore()
    for peer in peers:
        pl.semaphore_signal(barrier, inc=1, device_id=peer, device_id_type=MESH)

    copies = []

    def remote(source, target, peer):
        slot = len(copies)
        copy = pltpu.make_async_remote_copy(
            src_ref=source, dst_ref=target, send_sem=send_sems.at[slot], recv_sem=recv_sems.at[slot],
            device_id=peer, device_id_type=MESH,
        )
        copies.append(copy)
        return copy

    def exchange(stage, side):
        moves = []
        for quad, (rows, cols) in enumerate(((1, 1), (1, 0), (0, 1))):
            moves.append(remote(sent.at[stage, quad], landed.at[stage, quad], near(side * rows, side * cols)))
        return moves

    def fill(stage, order, values):
        for quad in range(4):
            rows = dot(order[quad * SLAB:(quad + 1) * SLAB, :], values).astype(BF16)
            if quad == 3:
                landed[stage, quad] = rows
            else:
                sent[stage, quad] = rows

    def arrived(stage, order):
        return dot(order[...], landed[stage].reshape(4 * SLAB, WIDTH))

    fill(0, nat2quad, x_ref[...])
    pl.semaphore_wait(barrier, len(peers))

    first = exchange(0, -1)
    for copy in first:
        copy.start()

    half = PIECE // 2
    ahead, behind = [], []
    for step in range(4):
        up = lax.rem(ring - step + RING, RING)
        down = lax.rem(ring + step, RING)
        if step == 0:
            ahead.append(remote(piece_hbm, wbuf.at[ring], ring_peer(1)))
            behind.append(remote(piece_hbm, wbuf.at[ring], ring_peer(RING - 1)))
        elif step < 3:
            ahead.append(remote(wbuf.at[up], wbuf.at[up], ring_peer(1)))
            behind.append(remote(wbuf.at[down], wbuf.at[down], ring_peer(RING - 1)))
        else:
            top, bottom = pl.ds(0, half), pl.ds(half, half)
            ahead.append(remote(wbuf.at[up, top], wbuf.at[up, top], ring_peer(1)))
            behind.append(remote(wbuf.at[down, bottom], wbuf.at[down, bottom], ring_peer(RING - 1)))

    def ring_step(step):
        if step > 0:
            ahead[step - 1].wait_recv()
            behind[step - 1].wait_recv()
        if step < 4:
            ahead[step].start()
            behind[step].start()

    spread = [remote(cot_hbm, cots.at[member], team_peer(step)) for step in range(1, TEAM)]
    for copy in spread:
        copy.start()
    ring_step(0)

    for copy in first:
        copy.wait_recv()
    values = arrived(0, quad2win)
    tokens[...] = values.astype(BF16)
    centered, inverse = stats(values)
    normed[...] = (centered * inverse).astype(BF16)
    loads[0].wait()
    for part in range(12):
        cols = slice(part * 256, (part + 1) * 256)
        packed[:, cols] = dot(normed[...], wqkv[:, cols]).astype(BF16)

    def attend_step(pair, carry):
        attend_pair(pair, is_last, table_ref, index_ref, packed, probs, attended)
        return carry

    ring_step(1)
    lax.fori_loop(0, PAIRS, attend_step, 0, unroll=PAIRS)
    ring_step(2)
    loads[1].wait()
    block = tokens[...].astype(F32) + dot(attended[...], wproj[...])
    fill(1, win2quad, block.astype(BF16))
    second = exchange(1, 1)
    for copy in second:
        copy.start()

    for copy in spread:
        copy.wait_recv()
    loads[2].wait()
    loads[3].wait()

    def merge_grad(spot):
        rows = dot(cots[...].reshape(TEAM * SLAB, OUT), wbuf[spot], LAST).astype(BF16)
        here = pl.ds(pl.multiple_of(spot * PIECE, PIECE), PIECE)
        gsend[:, :, here] = rows.reshape(TEAM, SLAB, PIECE)

    def merge_both(step):
        merge_grad(lax.rem(ring - step + RING, RING))
        merge_grad(lax.rem(ring + step, RING))

    merge_grad(ring)
    merge_both(1)
    merge_both(2)

    for copy in second:
        copy.wait_recv()
    slabs = arrived(1, quad2merge)
    parts = [slabs[spot * CELLS:(spot + 1) * CELLS] for spot in range(4)]
    total = sum(jnp.sum(part, axis=-1, keepdims=True) for part in parts)
    average = total * (1.0 / (4 * WIDTH))
    parts = [part - average for part in parts]
    total = sum(jnp.sum(part * part, axis=-1, keepdims=True) for part in parts)
    merge_inverse = lax.rsqrt(total * (1.0 / (4 * WIDTH)) + EPS)
    for spot in range(4):
        hat = parts[spot] * merge_inverse
        hats[spot] = hat
        rows = pad_rows(hat)
        for block_id in range(8):
            target = (2 * spot + block_id // 4) * PIECE
            msend[block_id % 4, :, target:target + PIECE] = rows[:, block_id * PIECE:(block_id + 1) * PIECE]
    mrecv[member] = msend[member]
    inputs = [
        remote(msend.at[lax.rem(member + step, TEAM)], mrecv.at[member], team_peer(step))
        for step in range(1, TEAM)
    ]
    for copy in inputs:
        copy.start()

    ring_step(3)
    merge_both(3)
    ring_step(4)
    merge_grad(lax.rem(ring + 4, RING))
    grecv[member] = gsend[member]
    grads = [
        remote(gsend.at[lax.rem(member + step, TEAM)], grecv.at[member], team_peer(step))
        for step in range(1, TEAM)
    ]
    for copy in grads:
        copy.start()

    for copy in inputs:
        copy.wait_recv()
    for part in range(8):
        cols = slice(part * 256, (part + 1) * 256)
        rows = dot(mrecv[...].reshape(TEAM * SLAB, WIDTH), wbuf[:, :, cols].reshape(RING * PIECE, 256))
        psend[:, :, cols] = rows.astype(BF16).reshape(TEAM, SLAB, 256)
    precv[member] = psend[member]

    for copy in grads:
        copy.wait_recv()
    slopes = []
    for spot in range(4):
        blocks = [
            grecv[block_id % 4, :, (2 * spot + block_id // 4) * PIECE:(2 * spot + block_id // 4 + 1) * PIECE]
            for block_id in range(8)
        ]
        slopes.append(jnp.concatenate(blocks, axis=1).astype(F32)[:CELLS])
    mean_slope = sum(jnp.sum(s, axis=-1, keepdims=True) for s in slopes) * (1.0 / (4 * WIDTH))
    mean_tilt = sum(
        jnp.sum(s * hats[spot], axis=-1, keepdims=True) for spot, s in enumerate(slopes)
    ) * (1.0 / (4 * WIDTH))
    slopes = [merge_inverse * (s - mean_slope - hats[spot] * mean_tilt) for spot, s in enumerate(slopes)]
    fill(2, merge2quad, jnp.concatenate(slopes, axis=0).astype(BF16))
    third = exchange(2, -1)
    for copy in third:
        copy.start()
    partials = [
        remote(psend.at[lax.rem(member + step, TEAM)], precv.at[member], team_peer(step))
        for step in range(1, TEAM)
    ]
    for copy in partials:
        copy.start()

    for copy in third:
        copy.wait_recv()
    attended[...] = arrived(2, quad2win).astype(BF16)
    datt[...] = dot(attended[...], wproj[...], LAST).astype(BF16)

    def unattend_step(pair, carry):
        unattend_pair(pair, packed, probs, datt, dpacked, dmain, dtail)
        return carry

    lax.fori_loop(0, PAIRS, unattend_step, 0, unroll=PAIRS)
    sum_team[member] = scatter_table(index_ref, dmain, dtail)
    team_sums = [remote(sum_team.at[member], sum_team.at[member], team_peer(step)) for step in range(1, TEAM)]
    for copy in team_sums:
        copy.start()

    dnormed = dot(dpacked[...], wqkv[...], LAST).astype(BF16).astype(F32)
    centered, inverse = stats(tokens[...].astype(F32))
    hat = centered * inverse
    slope = jnp.mean(dnormed * hat, axis=-1, keepdims=True)
    inner = inverse * (dnormed - jnp.mean(dnormed, axis=-1, keepdims=True) - hat * slope)
    fill(3, win2quad, (attended[...].astype(F32) + inner).astype(BF16))
    fourth = exchange(3, 1)
    for copy in fourth:
        copy.start()

    for copy in team_sums:
        copy.wait_recv()
    sum_ring[ring] = sum_team[0] + sum_team[1] + sum_team[2] + sum_team[3]
    ring_sums = [remote(sum_ring.at[ring], sum_ring.at[ring], ring_peer(step)) for step in range(1, RING)]
    for copy in ring_sums:
        copy.start()

    for copy in partials:
        copy.wait_recv()
    for part in range(8):
        cols = slice(part * 256, (part + 1) * 256)
        total = precv[0, :, cols].astype(F32)
        for peer in range(1, TEAM):
            total = total + precv[peer, :, cols].astype(F32)
        merged_ref[:, cols] = total.astype(BF16)

    for copy in ring_sums:
        copy.wait_recv()
    total = sum_ring[0]
    for peer in range(1, RING):
        total = total + sum_ring[peer]
    sum_bands[lat] = total
    band_sums = [remote(sum_bands.at[lat], sum_bands.at[lat], band_peer(step)) for step in range(1, BANDS)]
    for copy in band_sums:
        copy.start()

    for copy in fourth:
        copy.wait_recv()
    grad_ref[...] = arrived(3, quad2nat).astype(BF16)

    for copy in band_sums:
        copy.wait_recv()
    total = sum_bands[0]
    for peer in range(1, BANDS):
        total = total + sum_bands[peer]
    bias_ref[...] = total
    for copy in copies:
        copy.wait_send()


COPIES = 12 + 8 + 4 * 3 + 3 + 7 + 7


def fused(x, table, index, cot, piece, wqkv, wproj):
    consts = orders()
    vmem = pl.BlockSpec(memory_space=pltpu.VMEM)
    anywhere = pl.BlockSpec(memory_space=pl.ANY)
    return pl.pallas_call(
        kernel,
        out_shape=(
            jax.ShapeDtypeStruct((SLAB, OUT), BF16),
            jax.ShapeDtypeStruct((TOKENS, WIDTH), BF16),
            jax.ShapeDtypeStruct((HEADS, BUCKETS), F32),
        ),
        in_specs=[vmem] * 9 + [anywhere] * 4,
        out_specs=[vmem] * 3,
        scratch_shapes=[
            pltpu.VMEM((WIDTH, 3 * WIDTH), BF16),
            pltpu.VMEM((WIDTH, WIDTH), BF16),
            pltpu.VMEM((RING, PIECE, OUT), BF16),
            pltpu.VMEM((TEAM, SLAB, OUT), BF16),
            pltpu.VMEM((4, 3, SLAB, WIDTH), BF16),
            pltpu.VMEM((4, 4, SLAB, WIDTH), BF16),
            pltpu.VMEM((TOKENS, WIDTH), BF16),
            pltpu.VMEM((TOKENS, WIDTH), BF16),
            pltpu.VMEM((TOKENS, 3 * WIDTH), BF16),
            pltpu.VMEM((WINDOWS, HEADS, WINDOW, WINDOW), BF16),
            pltpu.VMEM((TOKENS, WIDTH), BF16),
            pltpu.VMEM((4, CELLS, WIDTH), F32),
            pltpu.VMEM((TEAM, SLAB, WIDTH), BF16),
            pltpu.VMEM((TEAM, SLAB, WIDTH), BF16),
            pltpu.VMEM((TEAM, SLAB, WIDTH), BF16),
            pltpu.VMEM((TEAM, SLAB, WIDTH), BF16),
            pltpu.VMEM((TEAM, SLAB, OUT), BF16),
            pltpu.VMEM((TEAM, SLAB, OUT), BF16),
            pltpu.VMEM((TOKENS, WIDTH), BF16),
            pltpu.VMEM((TOKENS, 3 * WIDTH), BF16),
            pltpu.VMEM((WINDOW * HEADS, LANES), F32),
            pltpu.VMEM((WINDOW * HEADS, LANES), F32),
            pltpu.VMEM((TEAM, HEADS, BUCKETS), F32),
            pltpu.VMEM((RING, HEADS, BUCKETS), F32),
            pltpu.VMEM((BANDS, HEADS, BUCKETS), F32),
            pltpu.SemaphoreType.DMA((4,)),
            pltpu.SemaphoreType.DMA((COPIES,)),
            pltpu.SemaphoreType.DMA((COPIES,)),
        ],
        compiler_params=pltpu.CompilerParams(
            collective_id=0, has_side_effects=True, vmem_limit_bytes=60 * 2**20
        ),
        name="fused_block",
    )(*consts, x, table, index, cot, piece, wqkv, wproj)


def shards(latents, qkv_weight, proj_weight, merge_weight, bias_table, bias_index, cotangent):
    table = jnp.pad(bias_table, ((0, 0), (0, BUCKETS - bias_table.shape[1])))
    index = jnp.pad(bias_index, ((0, 0), (0, 2 * LANES - WINDOW)))
    cot = jnp.pad(cotangent.reshape(CELLS, OUT), ((0, SLAB - CELLS), (0, 0)))
    merged, grad, grad_table = fused(
        latents.reshape(TOKENS, WIDTH), table, index, cot, merge_weight, qkv_weight, proj_weight
    )
    return (
        merged[:CELLS].reshape(cotangent.shape),
        grad.reshape(latents.shape),
        grad_table[:, :bias_table.shape[1]],
    )


def solution(mesh):
    return jax.shard_map(
        shards,
        mesh=mesh,
        in_specs=(
            P(None, "lat", "lon", None),
            P(),
            P(),
            P("lon", None),
            P(),
            P(),
            P(None, "lat", "lon", None),
        ),
        out_specs=(P(None, "lat", "lon", None), P(None, "lat", "lon", None), P()),
        check_vma=False,
    )
```

```python
import jax
import jax.numpy as jnp
import numpy as np
from jax import lax
from jax.experimental import pallas as pl
from jax.experimental.pallas import tpu as pltpu
from jax.sharding import PartitionSpec as P

EPS = 1e-05
MASKED = -1e30
HEADS = 16
PAIRS = 8
HEAD_DIM = 64
WINDOW = 144
WINDOWS = 2
TOKENS = WINDOW * WINDOWS
WIDTH = 1024
OUT = 2048
BUCKETS = 768
LANES = 128
SPLIT = 256
TEAM = 4
RING = 8
BANDS = 8
PIECE = 128
CELLS = 72
SLAB = 80
F32 = jnp.float32
BF16 = jnp.bfloat16
LAST = (((1,), (1,)), ((), ()))
FIRST = (((0,), (0,)), ((), ()))
MESH = pl.DeviceIdType.MESH


def dot(a, b, dims=(((1,), (0,)), ((), ()))):
    return lax.dot_general(a, b, dims, preferred_element_type=F32)


def lanes(start, size=LANES):
    return pl.ds(pl.multiple_of(start, LANES), size)


def quad_row(level, row, col):
    quad = 2 * (row // 6) + col // 3
    return quad * SLAB + level * 18 + (row % 6) * 3 + col % 3


def orders():
    natural = np.zeros((4 * SLAB, TOKENS), np.float32)
    window = np.zeros((TOKENS, 4 * SLAB), np.float32)
    merge = np.zeros((TOKENS, 4 * SLAB), np.float32)
    for level in range(4):
        for row in range(12):
            for col in range(6):
                cell = (level * 12 + row) * 6 + col
                place = quad_row(level, row, col)
                natural[place, (row * 6 + col) * 4 + level] = 1
                source = quad_row((level + 1) % 4, (row + 6) % 12, (col + 3) % 6)
                window[cell, source] = 1
                spot = 2 * (col % 2) + row % 2
                merge[spot * CELLS + (row // 2 * 3 + col // 2) * 4 + level, place] = 1
    return [jnp.asarray(m, BF16) for m in (natural, window, window.T, merge, merge.T, natural.T)]


def stats(values):
    average = jnp.mean(values, axis=-1, keepdims=True)
    centered = values - average
    variance = jnp.mean(centered * centered, axis=-1, keepdims=True)
    return centered, lax.rsqrt(variance + EPS)


def half_mask(shape, half):
    lane = lax.broadcasted_iota(jnp.int32, shape, 1)
    return (lane >= HEAD_DIM) if half else (lane < HEAD_DIM)


def region_code(shape, axis, window, is_last):
    token = lax.broadcasted_iota(jnp.int32, shape, axis)
    level = (token >= 72).astype(jnp.int32)
    row = token - 72 * level
    late = (row >= 36).astype(jnp.int32)
    return late * is_last + (2 * level if window == 1 else 0)


def allowed_pairs(window, is_last):
    shape = (WINDOW, WINDOW)
    return region_code(shape, 0, window, is_last) == region_code(shape, 1, window, is_last)


def gather_bias(table_ref, index_ref, head):
    tiles = []
    for tile in range(2):
        index = index_ref[:, tile * LANES:(tile + 1) * LANES]
        low = index & (LANES - 1)
        high = index >> 7
        found = None
        for chunk in range(BUCKETS // LANES):
            row = table_ref[head, chunk:chunk + 1, :]
            spread = jnp.broadcast_to(row, (WINDOW, LANES))
            part = jnp.take_along_axis(spread, low, axis=1, mode="promise_in_bounds")
            found = part if found is None else jnp.where(high == chunk, part, found)
        tiles.append(found)
    return jnp.concatenate(tiles, axis=1)[:, :WINDOW]


def attend_pair(pair, is_last, biases, packed, probs_ref, attended):
    base = pair * LANES
    bias = [biases[2 * pair + half] for half in range(2)]
    masks = [half_mask((WINDOW, LANES), half) for half in range(2)]
    zero = jnp.zeros((WINDOW, LANES), BF16)
    for window in range(WINDOWS):
        rows = slice(window * WINDOW, (window + 1) * WINDOW)
        allowed = allowed_pairs(window, is_last)
        query = packed[rows, lanes(base)] * jnp.array(HEAD_DIM ** -0.5, BF16)
        key = packed[rows, lanes(WIDTH + base)]
        value = packed[rows, lanes(2 * WIDTH + base)]
        mixed = None
        for half in range(2):
            scores = dot(jnp.where(masks[half], query, zero), key, LAST)
            scores = jnp.where(allowed, scores + bias[half], MASKED)
            weights = jnp.exp(scores - jnp.max(scores, axis=-1, keepdims=True))
            probs = (weights * (1.0 / jnp.sum(weights, axis=-1, keepdims=True))).astype(BF16)
            probs_ref[window, 2 * pair + half] = probs
            term = dot(probs, jnp.where(masks[half], value, zero))
            mixed = term if mixed is None else mixed + term
        attended[rows, lanes(base)] = mixed.astype(BF16)


def unattend_pair(pair, packed, probs_ref, datt, dpacked, dmain, dtail):
    base = pair * LANES
    scale = jnp.array(HEAD_DIM ** -0.5, BF16)
    masks = [half_mask((WINDOW, LANES), half) for half in range(2)]
    zero = jnp.zeros((WINDOW, LANES), BF16)
    sums = [None, None]
    for window in range(WINDOWS):
        rows = slice(window * WINDOW, (window + 1) * WINDOW)
        query = packed[rows, lanes(base)] * scale
        key = packed[rows, lanes(WIDTH + base)] * scale
        value = packed[rows, lanes(2 * WIDTH + base)]
        out_grad = datt[rows, lanes(base)]
        dquery, dkey, dvalue = None, None, None
        for half in range(2):
            grad = jnp.where(masks[half], out_grad, zero)
            probs = probs_ref[window, 2 * pair + half]
            wide = probs.astype(F32)
            product = wide * dot(grad, value, LAST)
            ds = product - wide * jnp.sum(product, axis=-1, keepdims=True)
            sums[half] = ds if sums[half] is None else sums[half] + ds
            narrow = ds.astype(BF16)
            one = dot(narrow, jnp.where(masks[half], key, zero))
            two = dot(narrow, jnp.where(masks[half], query, zero), FIRST)
            three = dot(probs, grad, FIRST)
            dquery = one if dquery is None else dquery + one
            dkey = two if dkey is None else dkey + two
            dvalue = three if dvalue is None else dvalue + three
        dpacked[rows, lanes(base)] = dquery.astype(BF16)
        dpacked[rows, lanes(WIDTH + base)] = dkey.astype(BF16)
        dpacked[rows, lanes(2 * WIDTH + base)] = dvalue.astype(BF16)
    for half in range(2):
        total = jnp.concatenate([sums[half], jnp.zeros((WINDOW, 2 * LANES - WINDOW), F32)], axis=1)
        for tile, store in enumerate((dmain, dtail)):
            cols = slice(tile * LANES, (tile + 1) * LANES)
            store[pl.ds(2 * pair + half, WINDOW, stride=HEADS), :] = total[:, cols]


def build_hots(index_ref, lows, hots):
    shape = (WINDOW, WINDOW)
    eye = lax.broadcasted_iota(jnp.int32, shape, 0) == lax.broadcasted_iota(jnp.int32, shape, 1)
    eye = jnp.where(eye, 1.0, 0.0).astype(BF16)
    low = (index_ref[:, :WINDOW] & (SPLIT - 1)).astype(F32).astype(BF16)
    flipped = dot(eye, low, LAST).astype(jnp.int32)
    lows[...] = jnp.concatenate([flipped, jnp.zeros((WINDOW, 2 * LANES - WINDOW), jnp.int32)], axis=1)
    bucket = lax.broadcasted_iota(jnp.int32, (WINDOW, SPLIT), 1)

    def build(tile):
        def step(row, carry):
            wanted = jnp.zeros((WINDOW, LANES), jnp.int32) + (row - tile * LANES)
            source = lows[:, tile * LANES:(tile + 1) * LANES]
            spread = jnp.take_along_axis(source, wanted, axis=1, mode="promise_in_bounds")
            spread = jnp.concatenate([spread, spread], axis=1)
            hots[row] = jnp.where(bucket == spread, 1.0, 0.0).astype(BF16)
            return carry

        return step

    lax.fori_loop(0, LANES, build(0), 0, unroll=4)
    lax.fori_loop(LANES, WINDOW, build(1), 0, unroll=4)


def scatter_table(index_ref, hots, dmain, dtail):
    def scatter_row(row, total):
        here = pl.ds(pl.multiple_of(row * HEADS, HEADS), HEADS)
        block = jnp.concatenate([dmain[here, :], dtail[here, :]], axis=1)[:, :WINDOW]
        high = index_ref[pl.ds(row, 1), :][:, :WINDOW] >> 8
        parts = jnp.concatenate(
            [jnp.where(high == part, block, 0.0) for part in range(BUCKETS // SPLIT)], axis=0
        )
        coarse = parts.astype(BF16)
        fine = (parts - coarse.astype(F32)).astype(BF16)
        return total + dot(jnp.concatenate([coarse, fine], axis=0), hots[row])

    rows = HEADS * (BUCKETS // SPLIT)
    total = lax.fori_loop(0, WINDOW, scatter_row, jnp.zeros((2 * rows, SPLIT), F32), unroll=8)
    total = total[:rows] + total[rows:]
    return jnp.concatenate([total[part * HEADS:(part + 1) * HEADS] for part in range(BUCKETS // SPLIT)], axis=1)


def pad_rows(values):
    return jnp.concatenate([values, jnp.zeros((SLAB - CELLS, values.shape[1]), F32)], axis=0).astype(BF16)


def kernel(
    nat2quad, quad2win, win2quad, quad2merge, merge2quad, quad2nat,
    x_ref, table_ref, raw_index, cot_ref, piece_hbm, wqkv_hbm, wproj_hbm,
    merged_ref, grad_ref, bias_ref,
    wqkv, wproj, wbuf, cots, sent, landed, tokens, normed, packed, probs, attended,
    hats, gsend, grecv, msend, mrecv, psend, precv, datt, dpacked, dmain, dtail,
    sum_team, sum_ring, sum_bands, chunks, index_ref, biases, lows, hots, local_sems, send_sems, recv_sems,
):
    lon = lax.axis_index("lon")
    lat = lax.axis_index("lat")
    ring = lon // TEAM
    member = lax.rem(lon, TEAM)
    lons = RING * TEAM
    is_last = (lat == BANDS - 1).astype(jnp.int32)

    def team_peer(step):
        return {"lon": ring * TEAM + lax.rem(member + step, TEAM), "lat": lat}

    def ring_peer(step):
        return {"lon": lax.rem(ring + step, RING) * TEAM + member, "lat": lat}

    def band_peer(step):
        return {"lon": lon, "lat": lax.rem(lat + step, BANDS)}

    def near(rows, cols):
        return {"lon": lax.rem(lon + cols + lons, lons), "lat": lax.rem(lat + rows + BANDS, BANDS)}

    peers = [team_peer(step) for step in range(1, TEAM)]
    peers += [ring_peer(step) for step in range(1, RING)]
    peers += [band_peer(step) for step in range(1, BANDS)]
    peers += [near(0, 1), near(0, -1), near(1, 1), near(-1, -1)]

    loads = [
        pltpu.make_async_copy(wqkv_hbm, wqkv, local_sems.at[0]),
        pltpu.make_async_copy(wproj_hbm, wproj, local_sems.at[1]),
        pltpu.make_async_copy(piece_hbm, wbuf.at[ring], local_sems.at[2]),
    ]
    for load in loads:
        load.start()

    barrier = pltpu.get_barrier_semaphore()
    for peer in peers:
        pl.semaphore_signal(barrier, inc=1, device_id=peer, device_id_type=MESH)

    copies = []

    def remote(source, target, peer):
        slot = len(copies)
        copy = pltpu.make_async_remote_copy(
            src_ref=source, dst_ref=target, send_sem=send_sems.at[slot], recv_sem=recv_sems.at[slot],
            device_id=peer, device_id_type=MESH,
        )
        copies.append(copy)
        return copy

    def exchange(stage, side):
        moves = []
        for quad, (rows, cols) in enumerate(((1, 1), (1, 0), (0, 1))):
            moves.append(remote(sent.at[stage, quad], landed.at[stage, quad], near(side * rows, side * cols)))
        return moves

    def fill(stage, order, values):
        for quad in range(4):
            rows = dot(order[quad * SLAB:(quad + 1) * SLAB, :], values).astype(BF16)
            if quad == 3:
                landed[stage, quad] = rows
            else:
                sent[stage, quad] = rows

    def arrived(stage, order):
        return dot(order[...], landed[stage].reshape(4 * SLAB, WIDTH))

    index_ref[...] = jnp.concatenate(
        [raw_index[...], jnp.zeros((WINDOW, 2 * LANES - WINDOW), jnp.int32)], axis=1
    )
    fill(0, nat2quad, x_ref[...].astype(F32).reshape(TOKENS, WIDTH).astype(BF16))
    cots[member] = pad_rows(cot_ref[...].astype(F32).reshape(CELLS, OUT))
    pl.semaphore_wait(barrier, len(peers))

    first = exchange(0, -1)
    for copy in first:
        copy.start()

    side = lax.rem(lat // 2, 2)
    quarter = PIECE // 4

    def share(part, count=1):
        return pl.ds(pl.multiple_of(side * (2 * quarter) + part * quarter, quarter), count * quarter)

    def above(step):
        return lax.rem(ring - step + RING, RING)

    def below(step):
        return lax.rem(ring + step, RING)

    ahead, behind, across = [], [], [[]]
    for step in range(4):
        if step == 0:
            ahead.append(remote(piece_hbm.at[share(0, 2)], wbuf.at[ring, share(0, 2)], ring_peer(1)))
            behind.append(remote(piece_hbm.at[share(0, 2)], wbuf.at[ring, share(0, 2)], ring_peer(RING - 1)))
        else:
            up = wbuf.at[above(step), share(0, 2 if step < 3 else 1)]
            down = wbuf.at[below(step), share(0, 2) if step < 3 else share(1)]
            ahead.append(remote(up, up, ring_peer(1)))
            behind.append(remote(down, down, ring_peer(RING - 1)))
    for step in range(1, 5):
        moves = []
        for spot in (above(step), below(step)) if step < 4 else (below(step),):
            for part, peer in ((0, band_peer(2)), (1, band_peer(BANDS - 2))):
                moves.append(remote(wbuf.at[spot, share(part)], wbuf.at[spot, share(part)], peer))
        across.append(moves)

    def ring_step(step):
        if step > 0:
            ahead[step - 1].wait_recv()
            behind[step - 1].wait_recv()
        if step < 4:
            ahead[step].start()
            behind[step].start()
        for copy in across[step]:
            copy.start()

    def across_wait(step):
        for copy in across[step]:
            copy.wait_recv()

    spread = [remote(cots.at[member], cots.at[member], team_peer(step)) for step in range(1, TEAM)]
    ring_step(0)

    for chunk in range(BUCKETS // LANES):
        cols = table_ref[:, chunk * LANES:min((chunk + 1) * LANES, table_ref.shape[1])]
        if cols.shape[1] < LANES:
            cols = jnp.concatenate([cols, jnp.zeros((HEADS, LANES - cols.shape[1]), F32)], axis=1)
        for head in range(HEADS):
            chunks[head, chunk:chunk + 1, :] = cols[head:head + 1, :]

    def bias_step(head, carry):
        biases[head] = gather_bias(chunks, index_ref, head)
        return carry

    lax.fori_loop(0, HEADS, bias_step, 0, unroll=4)

    for copy in first:
        copy.wait_recv()
    for copy in spread:
        copy.start()
    ring_step(1)
    values = arrived(0, quad2win)
    tokens[...] = values.astype(BF16)
    centered, inverse = stats(values)
    normed[...] = (centered * inverse).astype(BF16)
    loads[0].wait()
    for part in range(12):
        cols = slice(part * 256, (part + 1) * 256)
        packed[:, cols] = dot(normed[...], wqkv[:, cols]).astype(BF16)

    def attend_step(pair, carry):
        attend_pair(pair, is_last, biases, packed, probs, attended)
        return carry

    lax.fori_loop(0, PAIRS // 2, attend_step, 0, unroll=PAIRS // 2)
    ring_step(2)
    lax.fori_loop(PAIRS // 2, PAIRS, attend_step, 0, unroll=PAIRS // 2)
    loads[1].wait()
    block = tokens[...].astype(F32) + dot(attended[...], wproj[...])
    fill(1, win2quad, block.astype(BF16))
    second = exchange(1, 1)
    for copy in second:
        copy.start()

    for copy in spread:
        copy.wait_recv()
    loads[2].wait()

    def merge_grad(spot):
        rows = dot(cots[...].reshape(TEAM * SLAB, OUT), wbuf[spot], LAST).astype(BF16)
        here = pl.ds(pl.multiple_of(spot * PIECE, PIECE), PIECE)
        gsend[:, :, here] = rows.reshape(TEAM, SLAB, PIECE)

    def merge_both(step):
        merge_grad(above(step))
        merge_grad(below(step))

    merge_grad(ring)
    ring_step(3)
    across_wait(1)
    merge_both(1)
    across_wait(2)
    merge_both(2)
    ring_step(4)

    for copy in second:
        copy.wait_recv()
    slabs = arrived(1, quad2merge)
    parts = [slabs[spot * CELLS:(spot + 1) * CELLS] for spot in range(4)]
    total = sum(jnp.sum(part, axis=-1, keepdims=True) for part in parts)
    average = total * (1.0 / (4 * WIDTH))
    parts = [part - average for part in parts]
    total = sum(jnp.sum(part * part, axis=-1, keepdims=True) for part in parts)
    merge_inverse = lax.rsqrt(total * (1.0 / (4 * WIDTH)) + EPS)
    for spot in range(4):
        hat = parts[spot] * merge_inverse
        hats[spot] = hat
        rows = pad_rows(hat)
        for block_id in range(8):
            target = (2 * spot + block_id // 4) * PIECE
            msend[block_id % 4, :, target:target + PIECE] = rows[:, block_id * PIECE:(block_id + 1) * PIECE]
    mrecv[member] = msend[member]
    inputs = [
        remote(msend.at[lax.rem(member + step, TEAM)], mrecv.at[member], team_peer(step))
        for step in range(1, TEAM)
    ]
    for copy in inputs:
        copy.start()

    across_wait(3)
    merge_both(3)
    across_wait(4)
    merge_grad(below(4))
    grecv[member] = gsend[member]
    grads = [
        remote(gsend.at[lax.rem(member + step, TEAM)], grecv.at[member], team_peer(step))
        for step in range(1, TEAM)
    ]
    for copy in grads:
        copy.start()

    for copy in inputs:
        copy.wait_recv()
    for part in range(8):
        cols = slice(part * 256, (part + 1) * 256)
        rows = dot(mrecv[...].reshape(TEAM * SLAB, WIDTH), wbuf[:, :, cols].reshape(RING * PIECE, 256))
        psend[:, :, cols] = rows.astype(BF16).reshape(TEAM, SLAB, 256)
    precv[member] = psend[member]
    partials = [
        remote(psend.at[lax.rem(member + step, TEAM)], precv.at[member], team_peer(step))
        for step in range(1, TEAM)
    ]
    for copy in grads:
        copy.wait_recv()
    slopes = []
    for spot in range(4):
        blocks = [
            grecv[block_id % 4, :, (2 * spot + block_id // 4) * PIECE:(2 * spot + block_id // 4 + 1) * PIECE]
            for block_id in range(8)
        ]
        slopes.append(jnp.concatenate(blocks, axis=1).astype(F32)[:CELLS])
    mean_slope = sum(jnp.sum(s, axis=-1, keepdims=True) for s in slopes) * (1.0 / (4 * WIDTH))
    mean_tilt = sum(
        jnp.sum(s * hats[spot], axis=-1, keepdims=True) for spot, s in enumerate(slopes)
    ) * (1.0 / (4 * WIDTH))
    slopes = [merge_inverse * (s - mean_slope - hats[spot] * mean_tilt) for spot, s in enumerate(slopes)]
    fill(2, merge2quad, jnp.concatenate(slopes, axis=0).astype(BF16))
    third = exchange(2, -1)
    for copy in third:
        copy.start()
    build_hots(index_ref, lows, hots)
    for copy in third:
        copy.wait_recv()
    for copy in partials:
        copy.start()
    attended[...] = arrived(2, quad2win).astype(BF16)
    datt[...] = dot(attended[...], wproj[...], LAST).astype(BF16)

    def unattend_step(pair, carry):
        unattend_pair(pair, packed, probs, datt, dpacked, dmain, dtail)
        return carry

    lax.fori_loop(0, PAIRS, unattend_step, 0, unroll=PAIRS)
    sum_team[member] = scatter_table(index_ref, hots, dmain, dtail)
    team_sums = [remote(sum_team.at[member], sum_team.at[member], team_peer(step)) for step in range(1, TEAM)]
    for copy in team_sums:
        copy.start()

    dnormed = dot(dpacked[...], wqkv[...], LAST).astype(BF16).astype(F32)
    centered, inverse = stats(tokens[...].astype(F32))
    hat = centered * inverse
    slope = jnp.mean(dnormed * hat, axis=-1, keepdims=True)
    inner = inverse * (dnormed - jnp.mean(dnormed, axis=-1, keepdims=True) - hat * slope)
    fill(3, win2quad, (attended[...].astype(F32) + inner).astype(BF16))
    fourth = exchange(3, 1)
    for copy in fourth:
        copy.start()

    for copy in team_sums:
        copy.wait_recv()
    sum_ring[ring] = sum_team[0] + sum_team[1] + sum_team[2] + sum_team[3]
    ring_sums = [remote(sum_ring.at[ring], sum_ring.at[ring], ring_peer(step)) for step in range(1, RING)]
    for copy in ring_sums:
        copy.start()

    for copy in partials:
        copy.wait_recv()
    for part in range(8):
        cols = slice(part * 256, (part + 1) * 256)
        total = precv[0, :, cols].astype(F32)
        for peer in range(1, TEAM):
            total = total + precv[peer, :, cols].astype(F32)
        merged_ref[:, :, cols] = total[:CELLS].reshape(-1, 4, 256).astype(BF16)

    for copy in ring_sums:
        copy.wait_recv()
    total = sum_ring[0]
    for peer in range(1, RING):
        total = total + sum_ring[peer]
    sum_bands[lat] = total
    band_sums = [remote(sum_bands.at[lat], sum_bands.at[lat], band_peer(step)) for step in range(1, BANDS)]
    for copy in band_sums:
        copy.start()

    for copy in fourth:
        copy.wait_recv()
    grad_ref[...] = arrived(3, quad2nat).reshape(-1, 4, WIDTH).astype(BF16)

    for copy in band_sums:
        copy.wait_recv()
    total = sum_bands[0]
    for peer in range(1, BANDS):
        total = total + sum_bands[peer]
    bias_ref[...] = total[:, :bias_ref.shape[1]]
    for copy in copies:
        copy.wait_send()


COPIES = 12 + 8 + 14 + 4 * 3 + 3 + 7 + 7


def fused(x, table, index, cot, piece, wqkv, wproj):
    consts = orders()
    vmem = pl.BlockSpec(memory_space=pltpu.VMEM)
    anywhere = pl.BlockSpec(memory_space=pl.ANY)
    return pl.pallas_call(
        kernel,
        out_shape=(
            jax.ShapeDtypeStruct(cot.shape, BF16),
            jax.ShapeDtypeStruct(x.shape, BF16),
            jax.ShapeDtypeStruct(table.shape, F32),
        ),
        in_specs=[vmem] * 10 + [anywhere] * 3,
        out_specs=[vmem] * 3,
        scratch_shapes=[
            pltpu.VMEM((WIDTH, 3 * WIDTH), BF16),
            pltpu.VMEM((WIDTH, WIDTH), BF16),
            pltpu.VMEM((RING, PIECE, OUT), BF16),
            pltpu.VMEM((TEAM, SLAB, OUT), BF16),
            pltpu.VMEM((4, 3, SLAB, WIDTH), BF16),
            pltpu.VMEM((4, 4, SLAB, WIDTH), BF16),
            pltpu.VMEM((TOKENS, WIDTH), BF16),
            pltpu.VMEM((TOKENS, WIDTH), BF16),
            pltpu.VMEM((TOKENS, 3 * WIDTH), BF16),
            pltpu.VMEM((WINDOWS, HEADS, WINDOW, WINDOW), BF16),
            pltpu.VMEM((TOKENS, WIDTH), BF16),
            pltpu.VMEM((4, CELLS, WIDTH), F32),
            pltpu.VMEM((TEAM, SLAB, WIDTH), BF16),
            pltpu.VMEM((TEAM, SLAB, WIDTH), BF16),
            pltpu.VMEM((TEAM, SLAB, WIDTH), BF16),
            pltpu.VMEM((TEAM, SLAB, WIDTH), BF16),
            pltpu.VMEM((TEAM, SLAB, OUT), BF16),
            pltpu.VMEM((TEAM, SLAB, OUT), BF16),
            pltpu.VMEM((TOKENS, WIDTH), BF16),
            pltpu.VMEM((TOKENS, 3 * WIDTH), BF16),
            pltpu.VMEM((WINDOW * HEADS, LANES), F32),
            pltpu.VMEM((WINDOW * HEADS, LANES), F32),
            pltpu.VMEM((TEAM, HEADS, BUCKETS), F32),
            pltpu.VMEM((RING, HEADS, BUCKETS), F32),
            pltpu.VMEM((BANDS, HEADS, BUCKETS), F32),
            pltpu.VMEM((HEADS, 8, LANES), F32),
            pltpu.VMEM((WINDOW, 2 * LANES), jnp.int32),
            pltpu.VMEM((HEADS, WINDOW, WINDOW), F32),
            pltpu.VMEM((WINDOW, 2 * LANES), jnp.int32),
            pltpu.VMEM((WINDOW, WINDOW, SPLIT), BF16),
            pltpu.SemaphoreType.DMA((3,)),
            pltpu.SemaphoreType.DMA((COPIES,)),
            pltpu.SemaphoreType.DMA((COPIES,)),
        ],
        compiler_params=pltpu.CompilerParams(
            collective_id=0, has_side_effects=True, vmem_limit_bytes=60 * 2**20
        ),
        name="fused_block",
    )(*consts, x, table, index, cot, piece, wqkv, wproj)


def shards(latents, qkv_weight, proj_weight, merge_weight, bias_table, bias_index, cotangent):
    cot = cotangent.transpose(1, 2, 0, 3)
    cells = latents.transpose(1, 2, 0, 3)
    merged, grad, grad_table = fused(
        cells.reshape(-1, 4, WIDTH), bias_table, bias_index, cot.reshape(-1, 4, OUT), merge_weight, qkv_weight, proj_weight
    )
    return (
        merged.reshape(cot.shape).transpose(2, 0, 1, 3),
        grad.reshape(cells.shape).transpose(2, 0, 1, 3),
        grad_table,
    )


def solution(mesh):
    return jax.shard_map(
        shards,
        mesh=mesh,
        in_specs=(
            P(None, "lat", "lon", None),
            P(),
            P(),
            P("lon", None),
            P(),
            P(),
            P(None, "lat", "lon", None),
        ),
        out_specs=(P(None, "lat", "lon", None), P(None, "lat", "lon", None), P()),
        check_vma=False,
    )
```

```python
import jax
import jax.numpy as jnp
import numpy as np
from jax import lax
from jax.experimental import pallas as pl
from jax.experimental.pallas import tpu as pltpu
from jax.sharding import PartitionSpec as P

EPS = 1e-05
MASKED = -1e30
HEADS = 16
PAIRS = 8
HEAD_DIM = 64
WINDOW = 144
WINDOWS = 2
TOKENS = WINDOW * WINDOWS
WIDTH = 1024
OUT = 2048
BUCKETS = 768
LANES = 128
SPLIT = 256
TEAM = 4
RING = 8
BANDS = 8
PIECE = 128
CELLS = 72
SLAB = 80
HALF = 40
F32 = jnp.float32
BF16 = jnp.bfloat16
LAST = (((1,), (1,)), ((), ()))
FIRST = (((0,), (0,)), ((), ()))
MESH = pl.DeviceIdType.MESH


def dot(a, b, dims=(((1,), (0,)), ((), ()))):
    return lax.dot_general(a, b, dims, preferred_element_type=F32)


def lanes(start, size=LANES):
    return pl.ds(pl.multiple_of(start, LANES), size)


def quad_row(level, row, col):
    window, inner = divmod((level + 3) % 4, 2)
    quad = 2 * (row // 6) + col // 3
    return window * 4 * HALF + quad * HALF + inner * 18 + (row % 6) * 3 + col % 3


def orders():
    natural = np.zeros((8 * HALF, TOKENS), np.float32)
    window = np.zeros((TOKENS, 8 * HALF), np.float32)
    merge = np.zeros((TOKENS, 8 * HALF), np.float32)
    for level in range(4):
        for row in range(12):
            for col in range(6):
                cell = (level * 12 + row) * 6 + col
                place = quad_row(level, row, col)
                natural[place, (row * 6 + col) * 4 + level] = 1
                source = quad_row((level + 1) % 4, (row + 6) % 12, (col + 3) % 6)
                window[cell, source] = 1
                spot = 2 * (col % 2) + row % 2
                merge[spot * CELLS + (row // 2 * 3 + col // 2) * 4 + level, place] = 1
    window = window[:WINDOW, :4 * HALF]
    return [jnp.asarray(m, BF16) for m in (natural, window, window.T, merge, merge.T, natural.T)]


def stats(values):
    average = jnp.mean(values, axis=-1, keepdims=True)
    centered = values - average
    variance = jnp.mean(centered * centered, axis=-1, keepdims=True)
    return centered, lax.rsqrt(variance + EPS)


def half_mask(shape, half):
    lane = lax.broadcasted_iota(jnp.int32, shape, 1)
    return (lane >= HEAD_DIM) if half else (lane < HEAD_DIM)


def region_code(shape, axis, window, is_last):
    token = lax.broadcasted_iota(jnp.int32, shape, axis)
    level = (token >= 72).astype(jnp.int32)
    row = token - 72 * level
    late = (row >= 36).astype(jnp.int32)
    return late * is_last + (2 * level if window == 1 else 0)


def allowed_pairs(window, is_last):
    shape = (WINDOW, WINDOW)
    return region_code(shape, 0, window, is_last) == region_code(shape, 1, window, is_last)


def gather_bias(table_ref, index_ref, head):
    tiles = []
    for tile in range(2):
        index = index_ref[:, tile * LANES:(tile + 1) * LANES]
        low = index & (LANES - 1)
        high = index >> 7
        found = None
        for chunk in range(BUCKETS // LANES):
            row = table_ref[head, chunk:chunk + 1, :]
            spread = jnp.broadcast_to(row, (WINDOW, LANES))
            part = jnp.take_along_axis(spread, low, axis=1, mode="promise_in_bounds")
            found = part if found is None else jnp.where(high == chunk, part, found)
        tiles.append(found)
    return jnp.concatenate(tiles, axis=1)[:, :WINDOW]


def attend_pair(pair, window, is_last, biases, packed, probs_ref, attended):
    base = pair * LANES
    bias = [biases[2 * pair + half] for half in range(2)]
    masks = [half_mask((WINDOW, LANES), half) for half in range(2)]
    zero = jnp.zeros((WINDOW, LANES), BF16)
    rows = slice(window * WINDOW, (window + 1) * WINDOW)
    allowed = allowed_pairs(window, is_last)
    query = packed[rows, lanes(base)] * jnp.array(HEAD_DIM ** -0.5, BF16)
    key = packed[rows, lanes(WIDTH + base)]
    value = packed[rows, lanes(2 * WIDTH + base)]
    mixed = None
    for half in range(2):
        scores = dot(jnp.where(masks[half], query, zero), key, LAST)
        scores = jnp.where(allowed, scores + bias[half], MASKED)
        weights = jnp.exp(scores - jnp.max(scores, axis=-1, keepdims=True))
        probs = (weights * (1.0 / jnp.sum(weights, axis=-1, keepdims=True))).astype(BF16)
        probs_ref[window, 2 * pair + half] = probs
        term = dot(probs, jnp.where(masks[half], value, zero))
        mixed = term if mixed is None else mixed + term
    attended[rows, lanes(base)] = mixed.astype(BF16)


def unattend_pair(pair, window, packed, probs_ref, datt, dpacked, dmain, dtail):
    base = pair * LANES
    scale = jnp.array(HEAD_DIM ** -0.5, BF16)
    masks = [half_mask((WINDOW, LANES), half) for half in range(2)]
    zero = jnp.zeros((WINDOW, LANES), BF16)
    sums = [None, None]
    rows = slice(window * WINDOW, (window + 1) * WINDOW)
    query = packed[rows, lanes(base)] * scale
    key = packed[rows, lanes(WIDTH + base)] * scale
    value = packed[rows, lanes(2 * WIDTH + base)]
    out_grad = datt[rows, lanes(base)]
    dquery, dkey, dvalue = None, None, None
    for half in range(2):
        grad = jnp.where(masks[half], out_grad, zero)
        probs = probs_ref[window, 2 * pair + half]
        wide = probs.astype(F32)
        product = wide * dot(grad, value, LAST)
        ds = product - wide * jnp.sum(product, axis=-1, keepdims=True)
        sums[half] = ds
        narrow = ds.astype(BF16)
        one = dot(narrow, jnp.where(masks[half], key, zero))
        two = dot(narrow, jnp.where(masks[half], query, zero), FIRST)
        three = dot(probs, grad, FIRST)
        dquery = one if dquery is None else dquery + one
        dkey = two if dkey is None else dkey + two
        dvalue = three if dvalue is None else dvalue + three
    dpacked[rows, lanes(base)] = dquery.astype(BF16)
    dpacked[rows, lanes(WIDTH + base)] = dkey.astype(BF16)
    dpacked[rows, lanes(2 * WIDTH + base)] = dvalue.astype(BF16)
    for half in range(2):
        total = jnp.concatenate([sums[half], jnp.zeros((WINDOW, 2 * LANES - WINDOW), F32)], axis=1)
        for tile, store in enumerate((dmain, dtail)):
            cols = slice(tile * LANES, (tile + 1) * LANES)
            here = pl.ds(2 * pair + half, WINDOW, stride=HEADS)
            store[here, :] = total[:, cols] if window == 0 else store[here, :] + total[:, cols]


def build_hots(index_ref, lows, hots):
    shape = (WINDOW, WINDOW)
    eye = lax.broadcasted_iota(jnp.int32, shape, 0) == lax.broadcasted_iota(jnp.int32, shape, 1)
    eye = jnp.where(eye, 1.0, 0.0).astype(BF16)
    low = (index_ref[:, :WINDOW] & (SPLIT - 1)).astype(F32).astype(BF16)
    flipped = dot(eye, low, LAST).astype(jnp.int32)
    lows[...] = jnp.concatenate([flipped, jnp.zeros((WINDOW, 2 * LANES - WINDOW), jnp.int32)], axis=1)
    bucket = lax.broadcasted_iota(jnp.int32, (WINDOW, SPLIT), 1)

    def build(tile):
        def step(row, carry):
            wanted = jnp.zeros((WINDOW, LANES), jnp.int32) + (row - tile * LANES)
            source = lows[:, tile * LANES:(tile + 1) * LANES]
            spread = jnp.take_along_axis(source, wanted, axis=1, mode="promise_in_bounds")
            spread = jnp.concatenate([spread, spread], axis=1)
            hots[row] = jnp.where(bucket == spread, 1.0, 0.0).astype(BF16)
            return carry

        return step

    lax.fori_loop(0, LANES, build(0), 0, unroll=4)
    lax.fori_loop(LANES, WINDOW, build(1), 0, unroll=4)


def scatter_table(index_ref, hots, dmain, dtail):
    def scatter_row(row, total):
        here = pl.ds(pl.multiple_of(row * HEADS, HEADS), HEADS)
        block = jnp.concatenate([dmain[here, :], dtail[here, :]], axis=1)[:, :WINDOW]
        high = index_ref[pl.ds(row, 1), :][:, :WINDOW] >> 8
        parts = jnp.concatenate(
            [jnp.where(high == part, block, 0.0) for part in range(BUCKETS // SPLIT)], axis=0
        )
        coarse = parts.astype(BF16)
        fine = (parts - coarse.astype(F32)).astype(BF16)
        return total + dot(jnp.concatenate([coarse, fine], axis=0), hots[row])

    rows = HEADS * (BUCKETS // SPLIT)
    total = lax.fori_loop(0, WINDOW, scatter_row, jnp.zeros((2 * rows, SPLIT), F32), unroll=8)
    total = total[:rows] + total[rows:]
    return jnp.concatenate([total[part * HEADS:(part + 1) * HEADS] for part in range(BUCKETS // SPLIT)], axis=1)


def pad_rows(values):
    return jnp.concatenate([values, jnp.zeros((SLAB - CELLS, values.shape[1]), F32)], axis=0).astype(BF16)


def kernel(
    nat2quad, quad2win, win2quad, quad2merge, merge2quad, quad2nat,
    x_ref, table_ref, raw_index, cot_ref, piece_hbm, wqkv_hbm, wproj_hbm,
    merged_ref, grad_ref, bias_ref,
    wqkv, wproj, wbuf, cots, sent, landed, tokens, normed, packed, probs, attended,
    hats, gsend, grecv, msend, mrecv, psend, precv, datt, dpacked, dmain, dtail,
    sum_team, sum_ring, sum_bands, chunks, index_ref, biases, lows, hots, local_sems, send_sems, recv_sems,
):
    lon = lax.axis_index("lon")
    lat = lax.axis_index("lat")
    ring = lon // TEAM
    member = lax.rem(lon, TEAM)
    lons = RING * TEAM
    is_last = (lat == BANDS - 1).astype(jnp.int32)

    def team_peer(step):
        return {"lon": ring * TEAM + lax.rem(member + step, TEAM), "lat": lat}

    def ring_peer(step):
        return {"lon": lax.rem(ring + step, RING) * TEAM + member, "lat": lat}

    def band_peer(step):
        return {"lon": lon, "lat": lax.rem(lat + step, BANDS)}

    def near(rows, cols):
        return {"lon": lax.rem(lon + cols + lons, lons), "lat": lax.rem(lat + rows + BANDS, BANDS)}

    peers = [team_peer(step) for step in range(1, TEAM)]
    peers += [ring_peer(step) for step in range(1, RING)]
    peers += [band_peer(step) for step in range(1, BANDS)]
    peers += [near(0, 1), near(0, -1), near(1, 1), near(-1, -1)]

    loads = [
        pltpu.make_async_copy(wqkv_hbm, wqkv, local_sems.at[0]),
        pltpu.make_async_copy(wproj_hbm, wproj, local_sems.at[1]),
        pltpu.make_async_copy(piece_hbm, wbuf.at[ring], local_sems.at[2]),
    ]
    for load in loads:
        load.start()

    barrier = pltpu.get_barrier_semaphore()
    for peer in peers:
        pl.semaphore_signal(barrier, inc=1, device_id=peer, device_id_type=MESH)

    copies = []

    def remote(source, target, peer):
        slot = len(copies)
        copy = pltpu.make_async_remote_copy(
            src_ref=source, dst_ref=target, send_sem=send_sems.at[slot], recv_sem=recv_sems.at[slot],
            device_id=peer, device_id_type=MESH,
        )
        copies.append(copy)
        return copy

    def exchange(stage, side):
        moves = []
        for window in range(WINDOWS):
            moves.append([])
            for quad, (rows, cols) in enumerate(((1, 1), (1, 0), (0, 1))):
                source, target = sent.at[stage, window, quad], landed.at[stage, window, quad]
                moves[-1].append(remote(source, target, near(side * rows, side * cols)))
        return moves

    def fill(stage, window, order, values):
        rows = dot(order, values)
        for quad in range(4):
            part = rows[quad * HALF:(quad + 1) * HALF]
            part = jnp.concatenate([part[:, :WIDTH // 2], part[:, WIDTH // 2:]], axis=0).astype(BF16)
            if quad == 3:
                landed[stage, window, quad] = part
            else:
                sent[stage, window, quad] = part

    def fill_both(stage, order, values):
        for window in range(WINDOWS):
            fill(stage, window, order[window * 4 * HALF:(window + 1) * 4 * HALF, :], values)

    def halves(stage, window):
        block = landed[stage, window].astype(F32)
        rows = jnp.concatenate([block[:, :HALF], block[:, HALF:]], axis=2)
        return rows.reshape(4 * HALF, WIDTH).astype(BF16)

    def arrived(stage, window):
        return dot(quad2win[...], halves(stage, window))

    def arrived_both(stage, order):
        return dot(order[...], jnp.concatenate([halves(stage, window) for window in range(WINDOWS)], axis=0))

    def span(window):
        return slice(window * WINDOW, (window + 1) * WINDOW)

    index_ref[...] = jnp.concatenate(
        [raw_index[...], jnp.zeros((WINDOW, 2 * LANES - WINDOW), jnp.int32)], axis=1
    )
    fill_both(0, nat2quad, x_ref[...].astype(F32).reshape(TOKENS, WIDTH).astype(BF16))
    cots[member] = pad_rows(cot_ref[...].astype(F32).reshape(CELLS, OUT))
    pl.semaphore_wait(barrier, len(peers))

    first = exchange(0, -1)
    for copy in first[0] + first[1]:
        copy.start()

    side = lax.rem(lat // 2, 2)
    quarter = PIECE // 4

    def share(part, count=1):
        return pl.ds(pl.multiple_of(side * (2 * quarter) + part * quarter, quarter), count * quarter)

    def above(step):
        return lax.rem(ring - step + RING, RING)

    def below(step):
        return lax.rem(ring + step, RING)

    ahead, behind, across = [], [], [[]]
    for step in range(4):
        if step == 0:
            ahead.append(remote(piece_hbm.at[share(0, 2)], wbuf.at[ring, share(0, 2)], ring_peer(1)))
            behind.append(remote(piece_hbm.at[share(0, 2)], wbuf.at[ring, share(0, 2)], ring_peer(RING - 1)))
        else:
            up = wbuf.at[above(step), share(0, 2 if step < 3 else 1)]
            down = wbuf.at[below(step), share(0, 2) if step < 3 else share(1)]
            ahead.append(remote(up, up, ring_peer(1)))
            behind.append(remote(down, down, ring_peer(RING - 1)))
    for step in range(1, 5):
        moves = []
        for spot in (above(step), below(step)) if step < 4 else (below(step),):
            for part, peer in ((0, band_peer(2)), (1, band_peer(BANDS - 2))):
                moves.append(remote(wbuf.at[spot, share(part)], wbuf.at[spot, share(part)], peer))
        across.append(moves)

    def ring_step(step):
        if step > 0:
            ahead[step - 1].wait_recv()
            behind[step - 1].wait_recv()
        if step < 4:
            ahead[step].start()
            behind[step].start()
        for copy in across[step]:
            copy.start()

    def across_wait(step):
        for copy in across[step]:
            copy.wait_recv()

    spread = [remote(cots.at[member], cots.at[member], team_peer(step)) for step in range(1, TEAM)]
    ring_step(0)

    for chunk in range(BUCKETS // LANES):
        cols = table_ref[:, chunk * LANES:min((chunk + 1) * LANES, table_ref.shape[1])]
        if cols.shape[1] < LANES:
            cols = jnp.concatenate([cols, jnp.zeros((HEADS, LANES - cols.shape[1]), F32)], axis=1)
        for head in range(HEADS):
            chunks[head, chunk:chunk + 1, :] = cols[head:head + 1, :]

    def bias_step(head, carry):
        biases[head] = gather_bias(chunks, index_ref, head)
        return carry

    lax.fori_loop(0, HEADS, bias_step, 0, unroll=4)

    for copy in first[0] + first[1]:
        copy.wait_recv()
    for copy in spread:
        copy.start()
    ring_step(1)
    for window in range(WINDOWS):
        values = arrived(0, window)
        tokens[span(window), :] = values.astype(BF16)
        centered, inverse = stats(values)
        normed[span(window), :] = (centered * inverse).astype(BF16)
    loads[0].wait()
    for part in range(12):
        cols = slice(part * 256, (part + 1) * 256)
        packed[:, cols] = dot(normed[...], wqkv[:, cols]).astype(BF16)

    def attend_step(window):
        def step(pair, carry):
            attend_pair(pair, window, is_last, biases, packed, probs, attended)
            return carry

        return step

    second = exchange(1, 1)
    loads[1].wait()
    for window in range(WINDOWS):
        lax.fori_loop(0, PAIRS, attend_step(window), 0, unroll=PAIRS)
        rows = span(window)
        block = tokens[rows, :].astype(F32) + dot(attended[rows, :], wproj[...])
        fill(1, window, win2quad[...], block.astype(BF16))
        for copy in second[window]:
            copy.start()
        if window == 0:
            ring_step(2)

    for copy in spread:
        copy.wait_recv()
    loads[2].wait()

    def merge_grad(spot):
        rows = dot(cots[...].reshape(TEAM * SLAB, OUT), wbuf[spot], LAST).astype(BF16)
        here = pl.ds(pl.multiple_of(spot * PIECE, PIECE), PIECE)
        gsend[:, :, here] = rows.reshape(TEAM, SLAB, PIECE)

    def merge_both(step):
        merge_grad(above(step))
        merge_grad(below(step))

    merge_grad(ring)
    ring_step(3)
    across_wait(1)
    merge_both(1)
    across_wait(2)
    merge_both(2)
    ring_step(4)

    for copy in second[0] + second[1]:
        copy.wait_recv()
    slabs = arrived_both(1, quad2merge)
    parts = [slabs[spot * CELLS:(spot + 1) * CELLS] for spot in range(4)]
    total = sum(jnp.sum(part, axis=-1, keepdims=True) for part in parts)
    average = total * (1.0 / (4 * WIDTH))
    parts = [part - average for part in parts]
    total = sum(jnp.sum(part * part, axis=-1, keepdims=True) for part in parts)
    merge_inverse = lax.rsqrt(total * (1.0 / (4 * WIDTH)) + EPS)
    for spot in range(4):
        hat = parts[spot] * merge_inverse
        hats[spot] = hat
        rows = pad_rows(hat)
        for block_id in range(8):
            target = (2 * spot + block_id // 4) * PIECE
            msend[block_id % 4, :, target:target + PIECE] = rows[:, block_id * PIECE:(block_id + 1) * PIECE]
    mrecv[member] = msend[member]
    inputs = [
        remote(msend.at[lax.rem(member + step, TEAM)], mrecv.at[member], team_peer(step))
        for step in range(1, TEAM)
    ]
    for copy in inputs:
        copy.start()

    across_wait(3)
    merge_both(3)
    across_wait(4)
    merge_grad(below(4))
    grecv[member] = gsend[member]
    grads = [
        remote(gsend.at[lax.rem(member + step, TEAM)], grecv.at[member], team_peer(step))
        for step in range(1, TEAM)
    ]
    for copy in grads:
        copy.start()

    for copy in inputs:
        copy.wait_recv()
    for part in range(8):
        cols = slice(part * 256, (part + 1) * 256)
        rows = dot(mrecv[...].reshape(TEAM * SLAB, WIDTH), wbuf[:, :, cols].reshape(RING * PIECE, 256))
        psend[:, :, cols] = rows.astype(BF16).reshape(TEAM, SLAB, 256)
    precv[member] = psend[member]
    partials = [
        remote(psend.at[lax.rem(member + step, TEAM)], precv.at[member], team_peer(step))
        for step in range(1, TEAM)
    ]
    for copy in grads:
        copy.wait_recv()
    slopes = []
    for spot in range(4):
        blocks = [
            grecv[block_id % 4, :, (2 * spot + block_id // 4) * PIECE:(2 * spot + block_id // 4 + 1) * PIECE]
            for block_id in range(8)
        ]
        slopes.append(jnp.concatenate(blocks, axis=1).astype(F32)[:CELLS])
    mean_slope = sum(jnp.sum(s, axis=-1, keepdims=True) for s in slopes) * (1.0 / (4 * WIDTH))
    mean_tilt = sum(
        jnp.sum(s * hats[spot], axis=-1, keepdims=True) for spot, s in enumerate(slopes)
    ) * (1.0 / (4 * WIDTH))
    slopes = [merge_inverse * (s - mean_slope - hats[spot] * mean_tilt) for spot, s in enumerate(slopes)]
    fill_both(2, merge2quad, jnp.concatenate(slopes, axis=0).astype(BF16))
    third = exchange(2, -1)
    for copy in third[0] + third[1]:
        copy.start()
    build_hots(index_ref, lows, hots)

    def unattend_step(window):
        def step(pair, carry):
            unattend_pair(pair, window, packed, probs, datt, dpacked, dmain, dtail)
            return carry

        return step

    def unattend(window):
        for copy in third[window]:
            copy.wait_recv()
        rows = span(window)
        attended[rows, :] = arrived(2, window).astype(BF16)
        datt[rows, :] = dot(attended[rows, :], wproj[...], LAST).astype(BF16)
        lax.fori_loop(0, PAIRS, unattend_step(window), 0, unroll=PAIRS)

    fourth = exchange(3, 1)

    def finish(window):
        rows = span(window)
        dnormed = dot(dpacked[rows, :], wqkv[...], LAST).astype(BF16).astype(F32)
        centered, inverse = stats(tokens[rows, :].astype(F32))
        hat = centered * inverse
        slope = jnp.mean(dnormed * hat, axis=-1, keepdims=True)
        inner = inverse * (dnormed - jnp.mean(dnormed, axis=-1, keepdims=True) - hat * slope)
        fill(3, window, win2quad[...], (attended[rows, :].astype(F32) + inner).astype(BF16))
        for copy in fourth[window]:
            copy.start()

    unattend(0)
    finish(0)
    for copy in partials:
        copy.start()
    unattend(1)
    sum_team[member] = scatter_table(index_ref, hots, dmain, dtail)
    team_sums = [remote(sum_team.at[member], sum_team.at[member], team_peer(step)) for step in range(1, TEAM)]
    for copy in team_sums:
        copy.start()
    finish(1)

    for copy in team_sums:
        copy.wait_recv()
    sum_ring[ring] = sum_team[0] + sum_team[1] + sum_team[2] + sum_team[3]
    ring_sums = [remote(sum_ring.at[ring], sum_ring.at[ring], ring_peer(step)) for step in range(1, RING)]
    for copy in ring_sums:
        copy.start()

    for copy in partials:
        copy.wait_recv()
    for part in range(8):
        cols = slice(part * 256, (part + 1) * 256)
        total = precv[0, :, cols].astype(F32)
        for peer in range(1, TEAM):
            total = total + precv[peer, :, cols].astype(F32)
        merged_ref[:, cols] = total[:CELLS].astype(BF16)

    for copy in ring_sums:
        copy.wait_recv()
    total = sum_ring[0]
    for peer in range(1, RING):
        total = total + sum_ring[peer]
    sum_bands[lat] = total
    band_sums = [remote(sum_bands.at[lat], sum_bands.at[lat], band_peer(step)) for step in range(1, BANDS)]
    for copy in band_sums:
        copy.start()

    for copy in fourth[0] + fourth[1]:
        copy.wait_recv()
    grad_ref[...] = arrived_both(3, quad2nat).astype(BF16)

    for copy in band_sums:
        copy.wait_recv()
    total = sum_bands[0]
    for peer in range(1, BANDS):
        total = total + sum_bands[peer]
    bias_ref[...] = total[:, :bias_ref.shape[1]]
    for copy in copies:
        copy.wait_send()


COPIES = 24 + 8 + 14 + 4 * 3 + 3 + 7 + 7


def fused(x, table, index, cot, piece, wqkv, wproj):
    consts = orders()
    vmem = pl.BlockSpec(memory_space=pltpu.VMEM)
    anywhere = pl.BlockSpec(memory_space=pl.ANY)
    return pl.pallas_call(
        kernel,
        out_shape=(
            jax.ShapeDtypeStruct((CELLS, OUT), BF16),
            jax.ShapeDtypeStruct((TOKENS, WIDTH), BF16),
            jax.ShapeDtypeStruct(table.shape, F32),
        ),
        in_specs=[vmem] * 10 + [anywhere] * 3,
        out_specs=[vmem] * 3,
        scratch_shapes=[
            pltpu.VMEM((WIDTH, 3 * WIDTH), BF16),
            pltpu.VMEM((WIDTH, WIDTH), BF16),
            pltpu.VMEM((RING, PIECE, OUT), BF16),
            pltpu.VMEM((TEAM, SLAB, OUT), BF16),
            pltpu.VMEM((4, WINDOWS, 3, 2 * HALF, WIDTH // 2), BF16),
            pltpu.VMEM((4, WINDOWS, 4, 2 * HALF, WIDTH // 2), BF16),
            pltpu.VMEM((TOKENS, WIDTH), BF16),
            pltpu.VMEM((TOKENS, WIDTH), BF16),
            pltpu.VMEM((TOKENS, 3 * WIDTH), BF16),
            pltpu.VMEM((WINDOWS, HEADS, WINDOW, WINDOW), BF16),
            pltpu.VMEM((TOKENS, WIDTH), BF16),
            pltpu.VMEM((4, CELLS, WIDTH), F32),
            pltpu.VMEM((TEAM, SLAB, WIDTH), BF16),
            pltpu.VMEM((TEAM, SLAB, WIDTH), BF16),
            pltpu.VMEM((TEAM, SLAB, WIDTH), BF16),
            pltpu.VMEM((TEAM, SLAB, WIDTH), BF16),
            pltpu.VMEM((TEAM, SLAB, OUT), BF16),
            pltpu.VMEM((TEAM, SLAB, OUT), BF16),
            pltpu.VMEM((TOKENS, WIDTH), BF16),
            pltpu.VMEM((TOKENS, 3 * WIDTH), BF16),
            pltpu.VMEM((WINDOW * HEADS, LANES), F32),
            pltpu.VMEM((WINDOW * HEADS, LANES), F32),
            pltpu.VMEM((TEAM, HEADS, BUCKETS), F32),
            pltpu.VMEM((RING, HEADS, BUCKETS), F32),
            pltpu.VMEM((BANDS, HEADS, BUCKETS), F32),
            pltpu.VMEM((HEADS, 8, LANES), F32),
            pltpu.VMEM((WINDOW, 2 * LANES), jnp.int32),
            pltpu.VMEM((HEADS, WINDOW, WINDOW), F32),
            pltpu.VMEM((WINDOW, 2 * LANES), jnp.int32),
            pltpu.VMEM((WINDOW, WINDOW, SPLIT), BF16),
            pltpu.SemaphoreType.DMA((3,)),
            pltpu.SemaphoreType.DMA((COPIES,)),
            pltpu.SemaphoreType.DMA((COPIES,)),
        ],
        compiler_params=pltpu.CompilerParams(
            collective_id=0, has_side_effects=True, vmem_limit_bytes=60 * 2**20
        ),
        name="fused_block",
    )(*consts, x, table, index, cot, piece, wqkv, wproj)


def shards(latents, qkv_weight, proj_weight, merge_weight, bias_table, bias_index, cotangent):
    cot = cotangent.transpose(1, 2, 0, 3)
    cells = latents.transpose(1, 2, 0, 3)
    merged, grad, grad_table = fused(
        cells.reshape(-1, 4, WIDTH), bias_table, bias_index, cot.reshape(-1, 4, OUT), merge_weight, qkv_weight, proj_weight
    )
    return (
        merged.reshape(cot.shape).transpose(2, 0, 1, 3),
        grad.reshape(cells.shape).transpose(2, 0, 1, 3),
        grad_table,
    )


def solution(mesh):
    return jax.shard_map(
        shards,
        mesh=mesh,
        in_specs=(
            P(None, "lat", "lon", None),
            P(),
            P(),
            P("lon", None),
            P(),
            P(),
            P(None, "lat", "lon", None),
        ),
        out_specs=(P(None, "lat", "lon", None), P(None, "lat", "lon", None), P()),
        check_vma=False,
    )
```

```python
import jax
import jax.numpy as jnp
import numpy as np
from jax import lax
from jax.experimental import pallas as pl
from jax.experimental.pallas import tpu as pltpu
from jax.sharding import PartitionSpec as P

EPS = 1e-05
MASKED = -1e30
HEADS = 16
PAIRS = 8
HEAD_DIM = 64
WINDOW = 144
WINDOWS = 2
TOKENS = WINDOW * WINDOWS
WIDTH = 1024
OUT = 2048
BUCKETS = 768
LANES = 128
SPLIT = 256
TEAM = 4
RING = 8
BANDS = 8
PIECE = 128
CELLS = 72
SLAB = 80
F32 = jnp.float32
BF16 = jnp.bfloat16
LAST = (((1,), (1,)), ((), ()))
FIRST = (((0,), (0,)), ((), ()))
MESH = pl.DeviceIdType.MESH


def dot(a, b, dims=(((1,), (0,)), ((), ()))):
    return lax.dot_general(a, b, dims, preferred_element_type=F32)


def lanes(start, size=LANES):
    return pl.ds(pl.multiple_of(start, LANES), size)


def quad_row(level, row, col):
    quad = 2 * (row // 6) + col // 3
    return quad * CELLS + level * 18 + (row % 6) * 3 + col % 3


def orders():
    natural = np.zeros((TOKENS, TOKENS), np.float32)
    window = np.zeros((TOKENS, TOKENS), np.float32)
    merge = np.zeros((TOKENS, TOKENS), np.float32)
    for level in range(4):
        for row in range(12):
            for col in range(6):
                cell = (level * 12 + row) * 6 + col
                place = quad_row(level, row, col)
                natural[place, (row * 6 + col) * 4 + level] = 1
                source = quad_row((level + 1) % 4, (row + 6) % 12, (col + 3) % 6)
                window[cell, source] = 1
                spot = 2 * (col % 2) + row % 2
                merge[spot * CELLS + (row // 2 * 3 + col // 2) * 4 + level, place] = 1
    return [jnp.asarray(m, BF16) for m in (natural, window, window.T, merge, merge.T, natural.T)]


def stats(values):
    average = jnp.mean(values, axis=-1, keepdims=True)
    centered = values - average
    variance = jnp.mean(centered * centered, axis=-1, keepdims=True)
    return centered, lax.rsqrt(variance + EPS)


def half_mask(shape, half):
    lane = lax.broadcasted_iota(jnp.int32, shape, 1)
    return (lane >= HEAD_DIM) if half else (lane < HEAD_DIM)


def region_code(shape, axis, window, is_last):
    token = lax.broadcasted_iota(jnp.int32, shape, axis)
    level = (token >= 72).astype(jnp.int32)
    row = token - 72 * level
    late = (row >= 36).astype(jnp.int32)
    return late * is_last + (2 * level if window == 1 else 0)


def allowed_pairs(window, is_last):
    shape = (WINDOW, WINDOW)
    return region_code(shape, 0, window, is_last) == region_code(shape, 1, window, is_last)


def gather_bias(table_ref, index_ref, head):
    tiles = []
    for tile in range(2):
        index = index_ref[:, tile * LANES:(tile + 1) * LANES]
        low = index & (LANES - 1)
        high = index >> 7
        found = None
        for chunk in range(BUCKETS // LANES):
            row = table_ref[head, chunk:chunk + 1, :]
            spread = jnp.broadcast_to(row, (WINDOW, LANES))
            part = jnp.take_along_axis(spread, low, axis=1, mode="promise_in_bounds")
            found = part if found is None else jnp.where(high == chunk, part, found)
        tiles.append(found)
    return jnp.concatenate(tiles, axis=1)[:, :WINDOW]


def attend_pair(pair, is_last, biases, packed, probs_ref, attended):
    base = pair * LANES
    bias = [biases[2 * pair + half] for half in range(2)]
    masks = [half_mask((WINDOW, LANES), half) for half in range(2)]
    zero = jnp.zeros((WINDOW, LANES), BF16)
    for window in range(WINDOWS):
        rows = slice(window * WINDOW, (window + 1) * WINDOW)
        allowed = allowed_pairs(window, is_last)
        query = packed[rows, lanes(base)] * jnp.array(HEAD_DIM ** -0.5, BF16)
        key = packed[rows, lanes(WIDTH + base)]
        value = packed[rows, lanes(2 * WIDTH + base)]
        mixed = None
        for half in range(2):
            scores = dot(jnp.where(masks[half], query, zero), key, LAST)
            scores = jnp.where(allowed, scores + bias[half], MASKED)
            weights = jnp.exp(scores - jnp.max(scores, axis=-1, keepdims=True))
            probs = (weights * (1.0 / jnp.sum(weights, axis=-1, keepdims=True))).astype(BF16)
            probs_ref[window, 2 * pair + half] = probs
            term = dot(probs, jnp.where(masks[half], value, zero))
            mixed = term if mixed is None else mixed + term
        attended[rows, lanes(base)] = mixed.astype(BF16)


def unattend_pair(pair, packed, probs_ref, datt, dpacked, dmain, dtail):
    base = pair * LANES
    scale = jnp.array(HEAD_DIM ** -0.5, BF16)
    masks = [half_mask((WINDOW, LANES), half) for half in range(2)]
    zero = jnp.zeros((WINDOW, LANES), BF16)
    sums = [None, None]
    for window in range(WINDOWS):
        rows = slice(window * WINDOW, (window + 1) * WINDOW)
        query = packed[rows, lanes(base)] * scale
        key = packed[rows, lanes(WIDTH + base)] * scale
        value = packed[rows, lanes(2 * WIDTH + base)]
        out_grad = datt[rows, lanes(base)]
        dquery, dkey, dvalue = None, None, None
        for half in range(2):
            grad = jnp.where(masks[half], out_grad, zero)
            probs = probs_ref[window, 2 * pair + half]
            wide = probs.astype(F32)
            product = wide * dot(grad, value, LAST)
            ds = product - wide * jnp.sum(product, axis=-1, keepdims=True)
            sums[half] = ds if sums[half] is None else sums[half] + ds
            narrow = ds.astype(BF16)
            one = dot(narrow, jnp.where(masks[half], key, zero))
            two = dot(narrow, jnp.where(masks[half], query, zero), FIRST)
            three = dot(probs, grad, FIRST)
            dquery = one if dquery is None else dquery + one
            dkey = two if dkey is None else dkey + two
            dvalue = three if dvalue is None else dvalue + three
        dpacked[rows, lanes(base)] = dquery.astype(BF16)
        dpacked[rows, lanes(WIDTH + base)] = dkey.astype(BF16)
        dpacked[rows, lanes(2 * WIDTH + base)] = dvalue.astype(BF16)
    for half in range(2):
        total = jnp.concatenate([sums[half], jnp.zeros((WINDOW, 2 * LANES - WINDOW), F32)], axis=1)
        for tile, store in enumerate((dmain, dtail)):
            cols = slice(tile * LANES, (tile + 1) * LANES)
            store[pl.ds(2 * pair + half, WINDOW, stride=HEADS), :] = total[:, cols]


def build_hots(index_ref, lows, hots):
    shape = (WINDOW, WINDOW)
    eye = lax.broadcasted_iota(jnp.int32, shape, 0) == lax.broadcasted_iota(jnp.int32, shape, 1)
    eye = jnp.where(eye, 1.0, 0.0).astype(BF16)
    low = (index_ref[:, :WINDOW] & (SPLIT - 1)).astype(F32).astype(BF16)
    flipped = dot(eye, low, LAST).astype(jnp.int32)
    lows[...] = jnp.concatenate([flipped, jnp.zeros((WINDOW, 2 * LANES - WINDOW), jnp.int32)], axis=1)
    bucket = lax.broadcasted_iota(jnp.int32, (WINDOW, SPLIT), 1)

    def build(tile):
        def step(row, carry):
            wanted = jnp.zeros((WINDOW, LANES), jnp.int32) + (row - tile * LANES)
            source = lows[:, tile * LANES:(tile + 1) * LANES]
            spread = jnp.take_along_axis(source, wanted, axis=1, mode="promise_in_bounds")
            spread = jnp.concatenate([spread, spread], axis=1)
            hots[row] = jnp.where(bucket == spread, 1.0, 0.0).astype(BF16)
            return carry

        return step

    lax.fori_loop(0, LANES, build(0), 0, unroll=4)
    lax.fori_loop(LANES, WINDOW, build(1), 0, unroll=4)


def scatter_table(index_ref, hots, dmain, dtail):
    def scatter_row(row, total):
        here = pl.ds(pl.multiple_of(row * HEADS, HEADS), HEADS)
        block = jnp.concatenate([dmain[here, :], dtail[here, :]], axis=1)[:, :WINDOW]
        high = index_ref[pl.ds(row, 1), :][:, :WINDOW] >> 8
        parts = jnp.concatenate(
            [jnp.where(high == part, block, 0.0) for part in range(BUCKETS // SPLIT)], axis=0
        )
        coarse = parts.astype(BF16)
        fine = (parts - coarse.astype(F32)).astype(BF16)
        return total + dot(jnp.concatenate([coarse, fine], axis=0), hots[row])

    rows = HEADS * (BUCKETS // SPLIT)
    total = lax.fori_loop(0, WINDOW, scatter_row, jnp.zeros((2 * rows, SPLIT), F32), unroll=8)
    total = total[:rows] + total[rows:]
    return jnp.concatenate([total[part * HEADS:(part + 1) * HEADS] for part in range(BUCKETS // SPLIT)], axis=1)


def pad_rows(values):
    return jnp.concatenate([values, jnp.zeros((SLAB - CELLS, values.shape[1]), F32)], axis=0).astype(BF16)


def kernel(
    nat2quad, quad2win, win2quad, quad2merge, merge2quad, quad2nat,
    x_ref, table_ref, raw_index, cot_ref, piece_hbm, wqkv_hbm, wproj_hbm,
    merged_ref, grad_ref, bias_ref,
    wqkv, wproj, wbuf, cots, sent, landed, tokens, normed, packed, probs, attended,
    hats, gsend, grecv, msend, mrecv, psend, precv, datt, dpacked, dmain, dtail,
    sum_team, sum_ring, sum_bands, chunks, index_ref, biases, lows, hots, local_sems, send_sems, recv_sems,
):
    lon = lax.axis_index("lon")
    lat = lax.axis_index("lat")
    ring = lon // TEAM
    member = lax.rem(lon, TEAM)
    lons = RING * TEAM
    is_last = (lat == BANDS - 1).astype(jnp.int32)

    def team_peer(step):
        return {"lon": ring * TEAM + lax.rem(member + step, TEAM), "lat": lat}

    def ring_peer(step):
        return {"lon": lax.rem(ring + step, RING) * TEAM + member, "lat": lat}

    def band_peer(step):
        return {"lon": lon, "lat": lax.rem(lat + step, BANDS)}

    def near(rows, cols):
        return {"lon": lax.rem(lon + cols + lons, lons), "lat": lax.rem(lat + rows + BANDS, BANDS)}

    peers = [team_peer(step) for step in range(1, TEAM)]
    peers += [ring_peer(step) for step in range(1, RING)]
    peers += [band_peer(step) for step in range(1, BANDS)]
    peers += [near(0, 1), near(0, -1), near(1, 1), near(-1, -1)]

    loads = [
        pltpu.make_async_copy(wqkv_hbm, wqkv, local_sems.at[0]),
        pltpu.make_async_copy(wproj_hbm, wproj, local_sems.at[1]),
        pltpu.make_async_copy(piece_hbm, wbuf.at[ring], local_sems.at[2]),
    ]
    for load in loads:
        load.start()

    barrier = pltpu.get_barrier_semaphore()
    for peer in peers:
        pl.semaphore_signal(barrier, inc=1, device_id=peer, device_id_type=MESH)

    copies = []

    def remote(source, target, peer):
        slot = len(copies)
        copy = pltpu.make_async_remote_copy(
            src_ref=source, dst_ref=target, send_sem=send_sems.at[slot], recv_sem=recv_sems.at[slot],
            device_id=peer, device_id_type=MESH,
        )
        copies.append(copy)
        return copy

    def exchange(stage, side):
        moves = []
        for quad, (rows, cols) in enumerate(((1, 1), (1, 0), (0, 1))):
            moves.append(remote(sent.at[stage, quad], landed.at[stage, quad], near(side * rows, side * cols)))
        return moves

    def fill(stage, order, values):
        rows = dot(order[...], values)
        for quad in range(4):
            part = rows[quad * CELLS:(quad + 1) * CELLS]
            part = jnp.concatenate([part[:, :WIDTH // 2], part[:, WIDTH // 2:]], axis=0).astype(BF16)
            if quad == 3:
                landed[stage, quad] = part
            else:
                sent[stage, quad] = part

    def arrived(stage, order):
        block = landed[stage].astype(F32)
        rows = jnp.concatenate([block[:, :CELLS], block[:, CELLS:]], axis=2)
        return dot(order[...], rows.reshape(TOKENS, WIDTH).astype(BF16))

    index_ref[...] = jnp.concatenate(
        [raw_index[...], jnp.zeros((WINDOW, 2 * LANES - WINDOW), jnp.int32)], axis=1
    )
    fill(0, nat2quad, x_ref[...].astype(F32).reshape(TOKENS, WIDTH).astype(BF16))
    cots[member] = pad_rows(cot_ref[...].astype(F32).reshape(CELLS, OUT))
    pl.semaphore_wait(barrier, len(peers))

    first = exchange(0, -1)
    for copy in first:
        copy.start()

    side = lax.rem(lat // 2, 2)
    quarter = PIECE // 4

    def share(part, count=1):
        return pl.ds(pl.multiple_of(side * (2 * quarter) + part * quarter, quarter), count * quarter)

    def above(step):
        return lax.rem(ring - step + RING, RING)

    def below(step):
        return lax.rem(ring + step, RING)

    ahead, behind, across = [], [], [[]]
    for step in range(4):
        if step == 0:
            ahead.append(remote(piece_hbm.at[share(0, 2)], wbuf.at[ring, share(0, 2)], ring_peer(1)))
            behind.append(remote(piece_hbm.at[share(0, 2)], wbuf.at[ring, share(0, 2)], ring_peer(RING - 1)))
        else:
            up = wbuf.at[above(step), share(0, 2 if step < 3 else 1)]
            down = wbuf.at[below(step), share(0, 2) if step < 3 else share(1)]
            ahead.append(remote(up, up, ring_peer(1)))
            behind.append(remote(down, down, ring_peer(RING - 1)))
    for step in range(1, 5):
        moves = []
        for spot in (above(step), below(step)) if step < 4 else (below(step),):
            for part, peer in ((0, band_peer(2)), (1, band_peer(BANDS - 2))):
                moves.append(remote(wbuf.at[spot, share(part)], wbuf.at[spot, share(part)], peer))
        across.append(moves)

    def ring_step(step):
        if step > 0:
            ahead[step - 1].wait_recv()
            behind[step - 1].wait_recv()
        if step < 4:
            ahead[step].start()
            behind[step].start()
        for copy in across[step]:
            copy.start()

    def across_wait(step):
        for copy in across[step]:
            copy.wait_recv()

    spread = [remote(cots.at[member], cots.at[member], team_peer(step)) for step in range(1, TEAM)]
    ring_step(0)

    for chunk in range(BUCKETS // LANES):
        cols = table_ref[:, chunk * LANES:min((chunk + 1) * LANES, table_ref.shape[1])]
        if cols.shape[1] < LANES:
            cols = jnp.concatenate([cols, jnp.zeros((HEADS, LANES - cols.shape[1]), F32)], axis=1)
        for head in range(HEADS):
            chunks[head, chunk:chunk + 1, :] = cols[head:head + 1, :]

    def bias_step(head, carry):
        biases[head] = gather_bias(chunks, index_ref, head)
        return carry

    lax.fori_loop(0, HEADS, bias_step, 0, unroll=4)

    for copy in first:
        copy.wait_recv()
    for copy in spread:
        copy.start()
    ring_step(1)
    values = arrived(0, quad2win)
    tokens[...] = values.astype(BF16)
    centered, inverse = stats(values)
    normed[...] = (centered * inverse).astype(BF16)
    loads[0].wait()
    for part in range(12):
        cols = slice(part * 256, (part + 1) * 256)
        packed[:, cols] = dot(normed[...], wqkv[:, cols]).astype(BF16)

    def attend_step(pair, carry):
        attend_pair(pair, is_last, biases, packed, probs, attended)
        return carry

    lax.fori_loop(0, PAIRS // 2, attend_step, 0, unroll=PAIRS // 2)
    ring_step(2)
    lax.fori_loop(PAIRS // 2, PAIRS, attend_step, 0, unroll=PAIRS // 2)
    loads[1].wait()
    block = tokens[...].astype(F32) + dot(attended[...], wproj[...])
    fill(1, win2quad, block.astype(BF16))
    second = exchange(1, 1)
    for copy in second:
        copy.start()

    for copy in spread:
        copy.wait_recv()
    loads[2].wait()

    def merge_grad(spot):
        rows = dot(cots[...].reshape(TEAM * SLAB, OUT), wbuf[spot], LAST).astype(BF16)
        here = pl.ds(pl.multiple_of(spot * PIECE, PIECE), PIECE)
        gsend[:, :, here] = rows.reshape(TEAM, SLAB, PIECE)

    def merge_both(step):
        merge_grad(above(step))
        merge_grad(below(step))

    merge_grad(ring)
    ring_step(3)
    across_wait(1)
    merge_both(1)
    across_wait(2)
    merge_both(2)
    ring_step(4)

    for copy in second:
        copy.wait_recv()
    slabs = arrived(1, quad2merge)
    parts = [slabs[spot * CELLS:(spot + 1) * CELLS] for spot in range(4)]
    total = sum(jnp.sum(part, axis=-1, keepdims=True) for part in parts)
    average = total * (1.0 / (4 * WIDTH))
    parts = [part - average for part in parts]
    total = sum(jnp.sum(part * part, axis=-1, keepdims=True) for part in parts)
    merge_inverse = lax.rsqrt(total * (1.0 / (4 * WIDTH)) + EPS)
    for spot in range(4):
        hat = parts[spot] * merge_inverse
        hats[spot] = hat
        rows = pad_rows(hat)
        for block_id in range(8):
            target = (2 * spot + block_id // 4) * PIECE
            msend[block_id % 4, :, target:target + PIECE] = rows[:, block_id * PIECE:(block_id + 1) * PIECE]
    mrecv[member] = msend[member]
    inputs = [
        remote(msend.at[lax.rem(member + step, TEAM)], mrecv.at[member], team_peer(step))
        for step in range(1, TEAM)
    ]
    for copy in inputs:
        copy.start()

    across_wait(3)
    merge_both(3)
    across_wait(4)
    merge_grad(below(4))
    grecv[member] = gsend[member]
    grads = [
        remote(gsend.at[lax.rem(member + step, TEAM)], grecv.at[member], team_peer(step))
        for step in range(1, TEAM)
    ]
    for copy in grads:
        copy.start()

    for copy in inputs:
        copy.wait_recv()
    for part in range(8):
        cols = slice(part * 256, (part + 1) * 256)
        rows = dot(mrecv[...].reshape(TEAM * SLAB, WIDTH), wbuf[:, :, cols].reshape(RING * PIECE, 256))
        psend[:, :, cols] = rows.astype(BF16).reshape(TEAM, SLAB, 256)
    core = lax.rem(member, 2)
    home = member - core
    sibling = {"lon": ring * TEAM + home + 1 - core, "lat": lat}
    other = {"lon": ring * TEAM + 2 - home + core, "lat": lat}
    partials = [
        remote(psend.at[home + 1 - core], precv.at[0], sibling),
        remote(psend.at[2 - home + 1 - core], precv.at[1], sibling),
    ]
    for copy in partials:
        copy.start()
    for copy in grads:
        copy.wait_recv()
    slopes = []
    for spot in range(4):
        blocks = [
            grecv[block_id % 4, :, (2 * spot + block_id // 4) * PIECE:(2 * spot + block_id // 4 + 1) * PIECE]
            for block_id in range(8)
        ]
        slopes.append(jnp.concatenate(blocks, axis=1).astype(F32)[:CELLS])
    mean_slope = sum(jnp.sum(s, axis=-1, keepdims=True) for s in slopes) * (1.0 / (4 * WIDTH))
    mean_tilt = sum(
        jnp.sum(s * hats[spot], axis=-1, keepdims=True) for spot, s in enumerate(slopes)
    ) * (1.0 / (4 * WIDTH))
    slopes = [merge_inverse * (s - mean_slope - hats[spot] * mean_tilt) for spot, s in enumerate(slopes)]
    fill(2, merge2quad, jnp.concatenate(slopes, axis=0).astype(BF16))
    third = exchange(2, -1)
    for copy in third:
        copy.start()
    build_hots(index_ref, lows, hots)
    for copy in third:
        copy.wait_recv()
    for copy in partials:
        copy.wait_recv()
    precv[3] = (psend[2 - home + core].astype(F32) + precv[1].astype(F32)).astype(BF16)
    summed = remote(precv.at[3], precv.at[2], other)
    summed.start()
    attended[...] = arrived(2, quad2win).astype(BF16)
    datt[...] = dot(attended[...], wproj[...], LAST).astype(BF16)

    def unattend_step(pair, carry):
        unattend_pair(pair, packed, probs, datt, dpacked, dmain, dtail)
        return carry

    lax.fori_loop(0, PAIRS, unattend_step, 0, unroll=PAIRS)
    dnormed = dot(dpacked[...], wqkv[...], LAST).astype(BF16).astype(F32)
    centered, inverse = stats(tokens[...].astype(F32))
    hat = centered * inverse
    slope = jnp.mean(dnormed * hat, axis=-1, keepdims=True)
    inner = inverse * (dnormed - jnp.mean(dnormed, axis=-1, keepdims=True) - hat * slope)
    fill(3, win2quad, (attended[...].astype(F32) + inner).astype(BF16))
    fourth = exchange(3, 1)
    for copy in fourth:
        copy.start()

    sum_team[member] = scatter_table(index_ref, hots, dmain, dtail)
    team_sums = [remote(sum_team.at[member], sum_team.at[member], team_peer(step)) for step in range(1, TEAM)]
    for copy in team_sums:
        copy.start()

    summed.wait_recv()
    for part in range(8):
        cols = slice(part * 256, (part + 1) * 256)
        total = psend[member, :, cols].astype(F32)
        for peer in (0, 2):
            total = total + precv[peer, :, cols].astype(F32)
        merged_ref[:, :, cols] = total[:CELLS].reshape(-1, 4, 256).astype(BF16)

    for copy in team_sums:
        copy.wait_recv()
    sum_ring[ring] = sum_team[0] + sum_team[1] + sum_team[2] + sum_team[3]
    ring_sums = [remote(sum_ring.at[ring], sum_ring.at[ring], ring_peer(step)) for step in range(1, RING)]
    for copy in ring_sums:
        copy.start()

    for copy in fourth:
        copy.wait_recv()
    grad_ref[...] = arrived(3, quad2nat).reshape(-1, 4, WIDTH).astype(BF16)

    for copy in ring_sums:
        copy.wait_recv()
    total = sum_ring[0]
    for peer in range(1, RING):
        total = total + sum_ring[peer]
    sum_bands[lat] = total
    band_sums = [remote(sum_bands.at[lat], sum_bands.at[lat], band_peer(step)) for step in range(1, BANDS)]
    for copy in band_sums:
        copy.start()

    for copy in band_sums:
        copy.wait_recv()
    total = sum_bands[0]
    for peer in range(1, BANDS):
        total = total + sum_bands[peer]
    bias_ref[...] = total[:, :bias_ref.shape[1]]
    for copy in copies:
        copy.wait_send()


COPIES = 12 + 8 + 14 + 4 * 3 + 3 + 7 + 7


def fused(x, table, index, cot, piece, wqkv, wproj):
    consts = orders()
    vmem = pl.BlockSpec(memory_space=pltpu.VMEM)
    anywhere = pl.BlockSpec(memory_space=pl.ANY)
    return pl.pallas_call(
        kernel,
        out_shape=(
            jax.ShapeDtypeStruct(cot.shape, BF16),
            jax.ShapeDtypeStruct(x.shape, BF16),
            jax.ShapeDtypeStruct(table.shape, F32),
        ),
        in_specs=[vmem] * 10 + [anywhere] * 3,
        out_specs=[vmem] * 3,
        scratch_shapes=[
            pltpu.VMEM((WIDTH, 3 * WIDTH), BF16),
            pltpu.VMEM((WIDTH, WIDTH), BF16),
            pltpu.VMEM((RING, PIECE, OUT), BF16),
            pltpu.VMEM((TEAM, SLAB, OUT), BF16),
            pltpu.VMEM((4, 3, 2 * CELLS, WIDTH // 2), BF16),
            pltpu.VMEM((4, 4, 2 * CELLS, WIDTH // 2), BF16),
            pltpu.VMEM((TOKENS, WIDTH), BF16),
            pltpu.VMEM((TOKENS, WIDTH), BF16),
            pltpu.VMEM((TOKENS, 3 * WIDTH), BF16),
            pltpu.VMEM((WINDOWS, HEADS, WINDOW, WINDOW), BF16),
            pltpu.VMEM((TOKENS, WIDTH), BF16),
            pltpu.VMEM((4, CELLS, WIDTH), F32),
            pltpu.VMEM((TEAM, SLAB, WIDTH), BF16),
            pltpu.VMEM((TEAM, SLAB, WIDTH), BF16),
            pltpu.VMEM((TEAM, SLAB, WIDTH), BF16),
            pltpu.VMEM((TEAM, SLAB, WIDTH), BF16),
            pltpu.VMEM((TEAM, SLAB, OUT), BF16),
            pltpu.VMEM((TEAM, SLAB, OUT), BF16),
            pltpu.VMEM((TOKENS, WIDTH), BF16),
            pltpu.VMEM((TOKENS, 3 * WIDTH), BF16),
            pltpu.VMEM((WINDOW * HEADS, LANES), F32),
            pltpu.VMEM((WINDOW * HEADS, LANES), F32),
            pltpu.VMEM((TEAM, HEADS, BUCKETS), F32),
            pltpu.VMEM((RING, HEADS, BUCKETS), F32),
            pltpu.VMEM((BANDS, HEADS, BUCKETS), F32),
            pltpu.VMEM((HEADS, 8, LANES), F32),
            pltpu.VMEM((WINDOW, 2 * LANES), jnp.int32),
            pltpu.VMEM((HEADS, WINDOW, WINDOW), F32),
            pltpu.VMEM((WINDOW, 2 * LANES), jnp.int32),
            pltpu.VMEM((WINDOW, WINDOW, SPLIT), BF16),
            pltpu.SemaphoreType.DMA((3,)),
            pltpu.SemaphoreType.DMA((COPIES,)),
            pltpu.SemaphoreType.DMA((COPIES,)),
        ],
        compiler_params=pltpu.CompilerParams(
            collective_id=0, has_side_effects=True, vmem_limit_bytes=60 * 2**20
        ),
        name="fused_block",
    )(*consts, x, table, index, cot, piece, wqkv, wproj)


def shards(latents, qkv_weight, proj_weight, merge_weight, bias_table, bias_index, cotangent):
    cot = cotangent.transpose(1, 2, 0, 3)
    cells = latents.transpose(1, 2, 0, 3)
    merged, grad, grad_table = fused(
        cells.reshape(-1, 4, WIDTH), bias_table, bias_index, cot.reshape(-1, 4, OUT), merge_weight, qkv_weight, proj_weight
    )
    return (
        merged.reshape(cot.shape).transpose(2, 0, 1, 3),
        grad.reshape(cells.shape).transpose(2, 0, 1, 3),
        grad_table,
    )


def solution(mesh):
    return jax.shard_map(
        shards,
        mesh=mesh,
        in_specs=(
            P(None, "lat", "lon", None),
            P(),
            P(),
            P("lon", None),
            P(),
            P(),
            P(None, "lat", "lon", None),
        ),
        out_specs=(P(None, "lat", "lon", None), P(None, "lat", "lon", None), P()),
        check_vma=False,
    )
```

```python
import jax
import jax.numpy as jnp
import numpy as np
from jax import lax
from jax.experimental import pallas as pl
from jax.experimental.pallas import tpu as pltpu
from jax.sharding import PartitionSpec as P

EPS = 1e-05
MASKED = -1e30
HEADS = 16
PAIRS = 8
HEAD_DIM = 64
WINDOW = 144
WINDOWS = 2
TOKENS = WINDOW * WINDOWS
WIDTH = 1024
OUT = 2048
BUCKETS = 768
LANES = 128
SPLIT = 256
TEAM = 4
RING = 8
BANDS = 8
PIECE = 128
CELLS = 72
SLAB = 80
F32 = jnp.float32
BF16 = jnp.bfloat16
LAST = (((1,), (1,)), ((), ()))
FIRST = (((0,), (0,)), ((), ()))
MESH = pl.DeviceIdType.MESH


def dot(a, b, dims=(((1,), (0,)), ((), ()))):
    return lax.dot_general(a, b, dims, preferred_element_type=F32)


def lanes(start, size=LANES):
    return pl.ds(pl.multiple_of(start, LANES), size)


def quad_row(level, row, col):
    quad = 2 * (row // 6) + col // 3
    return quad * SLAB + level * 18 + (row % 6) * 3 + col % 3


def orders():
    natural = np.zeros((4 * SLAB, TOKENS), np.float32)
    window = np.zeros((TOKENS, 4 * SLAB), np.float32)
    merge = np.zeros((TOKENS, 4 * SLAB), np.float32)
    for level in range(4):
        for row in range(12):
            for col in range(6):
                cell = (level * 12 + row) * 6 + col
                place = quad_row(level, row, col)
                natural[place, (row * 6 + col) * 4 + level] = 1
                source = quad_row((level + 1) % 4, (row + 6) % 12, (col + 3) % 6)
                window[cell, source] = 1
                spot = 2 * (col % 2) + row % 2
                merge[spot * CELLS + (row // 2 * 3 + col // 2) * 4 + level, place] = 1
    return [jnp.asarray(m, BF16) for m in (natural, window, window.T, merge, merge.T, natural.T)]


def stats(values):
    average = jnp.mean(values, axis=-1, keepdims=True)
    centered = values - average
    variance = jnp.mean(centered * centered, axis=-1, keepdims=True)
    return centered, lax.rsqrt(variance + EPS)


def half_mask(shape, half):
    lane = lax.broadcasted_iota(jnp.int32, shape, 1)
    return (lane >= HEAD_DIM) if half else (lane < HEAD_DIM)


def region_code(shape, axis, window, is_last):
    token = lax.broadcasted_iota(jnp.int32, shape, axis)
    level = (token >= 72).astype(jnp.int32)
    row = token - 72 * level
    late = (row >= 36).astype(jnp.int32)
    return late * is_last + (2 * level if window == 1 else 0)


def allowed_pairs(window, is_last):
    shape = (WINDOW, WINDOW)
    return region_code(shape, 0, window, is_last) == region_code(shape, 1, window, is_last)


def gather_bias(table_ref, index_ref, head):
    tiles = []
    for tile in range(2):
        index = index_ref[:, tile * LANES:(tile + 1) * LANES]
        low = index & (LANES - 1)
        high = index >> 7
        found = None
        for chunk in range(BUCKETS // LANES):
            row = table_ref[head, chunk:chunk + 1, :]
            spread = jnp.broadcast_to(row, (WINDOW, LANES))
            part = jnp.take_along_axis(spread, low, axis=1, mode="promise_in_bounds")
            found = part if found is None else jnp.where(high == chunk, part, found)
        tiles.append(found)
    return jnp.concatenate(tiles, axis=1)[:, :WINDOW]


def attend_pair(pair, is_last, biases, packed, probs_ref, attended):
    base = pair * LANES
    bias = [biases[2 * pair + half] for half in range(2)]
    masks = [half_mask((WINDOW, LANES), half) for half in range(2)]
    zero = jnp.zeros((WINDOW, LANES), BF16)
    for window in range(WINDOWS):
        rows = slice(window * WINDOW, (window + 1) * WINDOW)
        allowed = allowed_pairs(window, is_last)
        query = packed[rows, lanes(base)] * jnp.array(HEAD_DIM ** -0.5, BF16)
        key = packed[rows, lanes(WIDTH + base)]
        value = packed[rows, lanes(2 * WIDTH + base)]
        mixed = None
        for half in range(2):
            scores = dot(jnp.where(masks[half], query, zero), key, LAST)
            scores = jnp.where(allowed, scores + bias[half], MASKED)
            weights = jnp.exp(scores - jnp.max(scores, axis=-1, keepdims=True))
            probs = (weights * (1.0 / jnp.sum(weights, axis=-1, keepdims=True))).astype(BF16)
            probs_ref[window, 2 * pair + half] = probs
            term = dot(probs, jnp.where(masks[half], value, zero))
            mixed = term if mixed is None else mixed + term
        attended[rows, lanes(base)] = mixed.astype(BF16)


def unattend_pair(pair, packed, probs_ref, datt, dpacked, dmain, dtail):
    base = pair * LANES
    scale = jnp.array(HEAD_DIM ** -0.5, BF16)
    masks = [half_mask((WINDOW, LANES), half) for half in range(2)]
    zero = jnp.zeros((WINDOW, LANES), BF16)
    sums = [None, None]
    for window in range(WINDOWS):
        rows = slice(window * WINDOW, (window + 1) * WINDOW)
        query = packed[rows, lanes(base)] * scale
        key = packed[rows, lanes(WIDTH + base)] * scale
        value = packed[rows, lanes(2 * WIDTH + base)]
        out_grad = datt[rows, lanes(base)]
        dquery, dkey, dvalue = None, None, None
        for half in range(2):
            grad = jnp.where(masks[half], out_grad, zero)
            probs = probs_ref[window, 2 * pair + half]
            wide = probs.astype(F32)
            product = wide * dot(grad, value, LAST)
            ds = product - wide * jnp.sum(product, axis=-1, keepdims=True)
            sums[half] = ds if sums[half] is None else sums[half] + ds
            narrow = ds.astype(BF16)
            one = dot(narrow, jnp.where(masks[half], key, zero))
            two = dot(narrow, jnp.where(masks[half], query, zero), FIRST)
            three = dot(probs, grad, FIRST)
            dquery = one if dquery is None else dquery + one
            dkey = two if dkey is None else dkey + two
            dvalue = three if dvalue is None else dvalue + three
        dpacked[rows, lanes(base)] = dquery.astype(BF16)
        dpacked[rows, lanes(WIDTH + base)] = dkey.astype(BF16)
        dpacked[rows, lanes(2 * WIDTH + base)] = dvalue.astype(BF16)
    for half in range(2):
        total = jnp.concatenate([sums[half], jnp.zeros((WINDOW, 2 * LANES - WINDOW), F32)], axis=1)
        for tile, store in enumerate((dmain, dtail)):
            cols = slice(tile * LANES, (tile + 1) * LANES)
            store[pl.ds(2 * pair + half, WINDOW, stride=HEADS), :] = total[:, cols]


def build_hots(index_ref, lows, hots):
    shape = (WINDOW, WINDOW)
    eye = lax.broadcasted_iota(jnp.int32, shape, 0) == lax.broadcasted_iota(jnp.int32, shape, 1)
    eye = jnp.where(eye, 1.0, 0.0).astype(BF16)
    low = (index_ref[:, :WINDOW] & (SPLIT - 1)).astype(F32).astype(BF16)
    flipped = dot(eye, low, LAST).astype(jnp.int32)
    lows[...] = jnp.concatenate([flipped, jnp.zeros((WINDOW, 2 * LANES - WINDOW), jnp.int32)], axis=1)
    bucket = lax.broadcasted_iota(jnp.int32, (WINDOW, SPLIT), 1)

    def build(tile):
        def step(row, carry):
            wanted = jnp.zeros((WINDOW, LANES), jnp.int32) + (row - tile * LANES)
            source = lows[:, tile * LANES:(tile + 1) * LANES]
            spread = jnp.take_along_axis(source, wanted, axis=1, mode="promise_in_bounds")
            spread = jnp.concatenate([spread, spread], axis=1)
            hots[row] = jnp.where(bucket == spread, 1.0, 0.0).astype(BF16)
            return carry

        return step

    lax.fori_loop(0, LANES, build(0), 0, unroll=4)
    lax.fori_loop(LANES, WINDOW, build(1), 0, unroll=4)


def scatter_table(index_ref, hots, dmain, dtail):
    def scatter_row(row, total):
        here = pl.ds(pl.multiple_of(row * HEADS, HEADS), HEADS)
        block = jnp.concatenate([dmain[here, :], dtail[here, :]], axis=1)[:, :WINDOW]
        high = index_ref[pl.ds(row, 1), :][:, :WINDOW] >> 8
        parts = jnp.concatenate(
            [jnp.where(high == part, block, 0.0) for part in range(BUCKETS // SPLIT)], axis=0
        )
        coarse = parts.astype(BF16)
        fine = (parts - coarse.astype(F32)).astype(BF16)
        return total + dot(jnp.concatenate([coarse, fine], axis=0), hots[row])

    rows = HEADS * (BUCKETS // SPLIT)
    total = lax.fori_loop(0, WINDOW, scatter_row, jnp.zeros((2 * rows, SPLIT), F32), unroll=8)
    total = total[:rows] + total[rows:]
    return jnp.concatenate([total[part * HEADS:(part + 1) * HEADS] for part in range(BUCKETS // SPLIT)], axis=1)


def pad_rows(values):
    return jnp.concatenate([values, jnp.zeros((SLAB - CELLS, values.shape[1]), F32)], axis=0).astype(BF16)


def kernel(
    nat2quad, quad2win, win2quad, quad2merge, merge2quad, quad2nat,
    x_ref, table_ref, raw_index, cot_ref, piece_hbm, wqkv_hbm, wproj_hbm,
    merged_ref, grad_ref, bias_ref,
    wqkv, wproj, wbuf, cots, sent, landed, tokens, normed, packed, probs, attended,
    hats, gsend, grecv, msend, mrecv, psend, precv, datt, dpacked, dmain, dtail,
    sum_team, sum_ring, sum_bands, chunks, index_ref, biases, lows, hots, local_sems, send_sems, recv_sems,
):
    lon = lax.axis_index("lon")
    lat = lax.axis_index("lat")
    ring = lon // TEAM
    member = lax.rem(lon, TEAM)
    lons = RING * TEAM
    is_last = (lat == BANDS - 1).astype(jnp.int32)

    def team_peer(step):
        return {"lon": ring * TEAM + lax.rem(member + step, TEAM), "lat": lat}

    def ring_peer(step):
        return {"lon": lax.rem(ring + step, RING) * TEAM + member, "lat": lat}

    def band_peer(step):
        return {"lon": lon, "lat": lax.rem(lat + step, BANDS)}

    def near(rows, cols):
        return {"lon": lax.rem(lon + cols + lons, lons), "lat": lax.rem(lat + rows + BANDS, BANDS)}

    peers = [team_peer(step) for step in range(1, TEAM)]
    peers += [ring_peer(step) for step in range(1, RING)]
    peers += [band_peer(step) for step in range(1, BANDS)]
    peers += [near(0, 1), near(0, -1), near(1, 1), near(-1, -1)]

    loads = [
        pltpu.make_async_copy(wqkv_hbm, wqkv, local_sems.at[0]),
        pltpu.make_async_copy(wproj_hbm, wproj, local_sems.at[1]),
        pltpu.make_async_copy(piece_hbm, wbuf.at[ring], local_sems.at[2]),
    ]
    for load in loads:
        load.start()

    barrier = pltpu.get_barrier_semaphore()
    for peer in peers:
        pl.semaphore_signal(barrier, inc=1, device_id=peer, device_id_type=MESH)

    copies = []

    def remote(source, target, peer):
        slot = len(copies)
        copy = pltpu.make_async_remote_copy(
            src_ref=source, dst_ref=target, send_sem=send_sems.at[slot], recv_sem=recv_sems.at[slot],
            device_id=peer, device_id_type=MESH,
        )
        copies.append(copy)
        return copy

    def exchange(stage, side):
        moves = []
        for quad, (rows, cols) in enumerate(((1, 1), (1, 0), (0, 1))):
            moves.append(remote(sent.at[stage, quad], landed.at[stage, quad], near(side * rows, side * cols)))
        return moves

    def fill(stage, order, values):
        for quad in range(4):
            rows = dot(order[quad * SLAB:(quad + 1) * SLAB, :], values).astype(BF16)
            if quad == 3:
                landed[stage, quad] = rows
            else:
                sent[stage, quad] = rows

    def arrived(stage, order):
        return dot(order[...], landed[stage].reshape(4 * SLAB, WIDTH))

    index_ref[...] = jnp.concatenate(
        [raw_index[...], jnp.zeros((WINDOW, 2 * LANES - WINDOW), jnp.int32)], axis=1
    )
    fill(0, nat2quad, x_ref[...].astype(F32).reshape(TOKENS, WIDTH).astype(BF16))
    cots[member] = pad_rows(cot_ref[...].astype(F32).reshape(CELLS, OUT))
    pl.semaphore_wait(barrier, len(peers))

    first = exchange(0, -1)
    for copy in first:
        copy.start()

    side = lax.rem(lat // 2, 2)
    quarter = PIECE // 4

    def share(part, count=1):
        return pl.ds(pl.multiple_of(side * (2 * quarter) + part * quarter, quarter), count * quarter)

    def above(step):
        return lax.rem(ring - step + RING, RING)

    def below(step):
        return lax.rem(ring + step, RING)

    ahead, behind, across = [], [], [[]]
    for step in range(4):
        if step == 0:
            ahead.append(remote(piece_hbm.at[share(0, 2)], wbuf.at[ring, share(0, 2)], ring_peer(1)))
            behind.append(remote(piece_hbm.at[share(0, 2)], wbuf.at[ring, share(0, 2)], ring_peer(RING - 1)))
        else:
            up = wbuf.at[above(step), share(0, 2 if step < 3 else 1)]
            down = wbuf.at[below(step), share(0, 2) if step < 3 else share(1)]
            ahead.append(remote(up, up, ring_peer(1)))
            behind.append(remote(down, down, ring_peer(RING - 1)))
    for step in range(1, 5):
        moves = []
        for spot in (above(step), below(step)) if step < 4 else (below(step),):
            for part, peer in ((0, band_peer(2)), (1, band_peer(BANDS - 2))):
                moves.append(remote(wbuf.at[spot, share(part)], wbuf.at[spot, share(part)], peer))
        across.append(moves)

    def ring_step(step):
        if step > 0:
            ahead[step - 1].wait_recv()
            behind[step - 1].wait_recv()
        if step < 4:
            ahead[step].start()
            behind[step].start()
        for copy in across[step]:
            copy.start()

    def across_wait(step):
        for copy in across[step]:
            copy.wait_recv()

    spread = [remote(cots.at[member], cots.at[member], team_peer(step)) for step in range(1, TEAM)]
    ring_step(0)

    for chunk in range(BUCKETS // LANES):
        cols = table_ref[:, chunk * LANES:min((chunk + 1) * LANES, table_ref.shape[1])]
        if cols.shape[1] < LANES:
            cols = jnp.concatenate([cols, jnp.zeros((HEADS, LANES - cols.shape[1]), F32)], axis=1)
        for head in range(HEADS):
            chunks[head, chunk:chunk + 1, :] = cols[head:head + 1, :]

    def bias_step(head, carry):
        biases[head] = gather_bias(chunks, index_ref, head)
        return carry

    lax.fori_loop(0, HEADS, bias_step, 0, unroll=4)

    for copy in first:
        copy.wait_recv()
    for copy in spread:
        copy.start()
    ring_step(1)
    values = arrived(0, quad2win)
    tokens[...] = values.astype(BF16)
    centered, inverse = stats(values)
    normed[...] = (centered * inverse).astype(BF16)
    loads[0].wait()
    for part in range(12):
        cols = slice(part * 256, (part + 1) * 256)
        packed[:, cols] = dot(normed[...], wqkv[:, cols]).astype(BF16)

    def attend_step(pair, carry):
        attend_pair(pair, is_last, biases, packed, probs, attended)
        return carry

    lax.fori_loop(0, PAIRS // 2, attend_step, 0, unroll=PAIRS // 2)
    ring_step(2)
    lax.fori_loop(PAIRS // 2, PAIRS, attend_step, 0, unroll=PAIRS // 2)
    loads[1].wait()
    block = tokens[...].astype(F32) + dot(attended[...], wproj[...])
    fill(1, win2quad, block.astype(BF16))
    second = exchange(1, 1)
    for copy in second:
        copy.start()

    for copy in spread:
        copy.wait_recv()
    loads[2].wait()

    def merge_grad(spot):
        rows = dot(cots[...].reshape(TEAM * SLAB, OUT), wbuf[spot], LAST).astype(BF16)
        here = pl.ds(pl.multiple_of(spot * PIECE, PIECE), PIECE)
        gsend[:, :, here] = rows.reshape(TEAM, SLAB, PIECE)

    def merge_both(step):
        merge_grad(above(step))
        merge_grad(below(step))

    merge_grad(ring)
    ring_step(3)
    across_wait(1)
    merge_both(1)
    across_wait(2)
    merge_both(2)
    ring_step(4)

    for copy in second:
        copy.wait_recv()
    slabs = arrived(1, quad2merge)
    parts = [slabs[spot * CELLS:(spot + 1) * CELLS] for spot in range(4)]
    total = sum(jnp.sum(part, axis=-1, keepdims=True) for part in parts)
    average = total * (1.0 / (4 * WIDTH))
    parts = [part - average for part in parts]
    total = sum(jnp.sum(part * part, axis=-1, keepdims=True) for part in parts)
    merge_inverse = lax.rsqrt(total * (1.0 / (4 * WIDTH)) + EPS)
    for spot in range(4):
        hat = parts[spot] * merge_inverse
        hats[spot] = hat
        rows = pad_rows(hat)
        for block_id in range(8):
            target = (2 * spot + block_id // 4) * PIECE
            msend[block_id % 4, :, target:target + PIECE] = rows[:, block_id * PIECE:(block_id + 1) * PIECE]
    mrecv[member] = msend[member]
    inputs = [
        remote(msend.at[lax.rem(member + step, TEAM)], mrecv.at[member], team_peer(step))
        for step in range(1, TEAM)
    ]
    for copy in inputs:
        copy.start()

    across_wait(3)
    merge_both(3)
    across_wait(4)
    merge_grad(below(4))
    grecv[member] = gsend[member]
    grads = [
        remote(gsend.at[lax.rem(member + step, TEAM)], grecv.at[member], team_peer(step))
        for step in range(1, TEAM)
    ]
    for copy in grads:
        copy.start()

    for copy in inputs:
        copy.wait_recv()
    for part in range(8):
        cols = slice(part * 256, (part + 1) * 256)
        rows = dot(mrecv[...].reshape(TEAM * SLAB, WIDTH), wbuf[:, :, cols].reshape(RING * PIECE, 256))
        psend[:, :, cols] = rows.astype(BF16).reshape(TEAM, SLAB, 256)
    core = lax.rem(member, 2)
    home = member - core
    sibling = {"lon": ring * TEAM + home + 1 - core, "lat": lat}
    other = {"lon": ring * TEAM + 2 - home + core, "lat": lat}
    partials = [
        remote(psend.at[home + 1 - core], precv.at[0], sibling),
        remote(psend.at[2 - home + 1 - core], precv.at[1], sibling),
    ]
    for copy in partials:
        copy.start()
    for copy in grads:
        copy.wait_recv()
    slopes = []
    for spot in range(4):
        blocks = [
            grecv[block_id % 4, :, (2 * spot + block_id // 4) * PIECE:(2 * spot + block_id // 4 + 1) * PIECE]
            for block_id in range(8)
        ]
        slopes.append(jnp.concatenate(blocks, axis=1).astype(F32)[:CELLS])
    mean_slope = sum(jnp.sum(s, axis=-1, keepdims=True) for s in slopes) * (1.0 / (4 * WIDTH))
    mean_tilt = sum(
        jnp.sum(s * hats[spot], axis=-1, keepdims=True) for spot, s in enumerate(slopes)
    ) * (1.0 / (4 * WIDTH))
    slopes = [merge_inverse * (s - mean_slope - hats[spot] * mean_tilt) for spot, s in enumerate(slopes)]
    fill(2, merge2quad, jnp.concatenate(slopes, axis=0).astype(BF16))
    third = exchange(2, -1)
    for copy in third:
        copy.start()
    build_hots(index_ref, lows, hots)
    for copy in third:
        copy.wait_recv()
    for copy in partials:
        copy.wait_recv()
    precv[3] = (psend[2 - home + core].astype(F32) + precv[1].astype(F32)).astype(BF16)
    summed = remote(precv.at[3], precv.at[2], other)
    summed.start()
    attended[...] = arrived(2, quad2win).astype(BF16)
    datt[...] = dot(attended[...], wproj[...], LAST).astype(BF16)

    def unattend_step(pair, carry):
        unattend_pair(pair, packed, probs, datt, dpacked, dmain, dtail)
        return carry

    lax.fori_loop(0, PAIRS, unattend_step, 0, unroll=PAIRS)
    dnormed = dot(dpacked[...], wqkv[...], LAST).astype(BF16).astype(F32)
    centered, inverse = stats(tokens[...].astype(F32))
    hat = centered * inverse
    slope = jnp.mean(dnormed * hat, axis=-1, keepdims=True)
    inner = inverse * (dnormed - jnp.mean(dnormed, axis=-1, keepdims=True) - hat * slope)
    fill(3, win2quad, (attended[...].astype(F32) + inner).astype(BF16))
    fourth = exchange(3, 1)
    for copy in fourth:
        copy.start()

    sum_team[member] = scatter_table(index_ref, hots, dmain, dtail)
    team_sums = [remote(sum_team.at[member], sum_team.at[member], team_peer(step)) for step in range(1, TEAM)]
    for copy in team_sums:
        copy.start()

    summed.wait_recv()
    for part in range(8):
        cols = slice(part * 256, (part + 1) * 256)
        total = psend[member, :, cols].astype(F32)
        for peer in (0, 2):
            total = total + precv[peer, :, cols].astype(F32)
        merged_ref[:, :, cols] = total[:CELLS].reshape(-1, 4, 256).astype(BF16)

    for copy in team_sums:
        copy.wait_recv()
    sum_ring[ring] = sum_team[0] + sum_team[1] + sum_team[2] + sum_team[3]
    ring_sums = [remote(sum_ring.at[ring], sum_ring.at[ring], ring_peer(step)) for step in range(1, RING)]
    for copy in ring_sums:
        copy.start()

    for copy in fourth:
        copy.wait_recv()
    grad_ref[...] = arrived(3, quad2nat).reshape(-1, 4, WIDTH).astype(BF16)

    for copy in ring_sums:
        copy.wait_recv()
    total = sum_ring[0]
    for peer in range(1, RING):
        total = total + sum_ring[peer]
    sum_bands[lat] = total
    band_sums = [remote(sum_bands.at[lat], sum_bands.at[lat], band_peer(step)) for step in range(1, BANDS)]
    for copy in band_sums:
        copy.start()

    for copy in band_sums:
        copy.wait_recv()
    total = sum_bands[0]
    for peer in range(1, BANDS):
        total = total + sum_bands[peer]
    bias_ref[...] = total[:, :bias_ref.shape[1]]
    for copy in copies:
        copy.wait_send()


COPIES = 12 + 8 + 14 + 4 * 3 + 3 + 7 + 7


def fused(x, table, index, cot, piece, wqkv, wproj):
    consts = orders()
    vmem = pl.BlockSpec(memory_space=pltpu.VMEM)
    anywhere = pl.BlockSpec(memory_space=pl.ANY)
    return pl.pallas_call(
        kernel,
        out_shape=(
            jax.ShapeDtypeStruct(cot.shape, BF16),
            jax.ShapeDtypeStruct(x.shape, BF16),
            jax.ShapeDtypeStruct(table.shape, F32),
        ),
        in_specs=[vmem] * 10 + [anywhere] * 3,
        out_specs=[vmem] * 3,
        scratch_shapes=[
            pltpu.VMEM((WIDTH, 3 * WIDTH), BF16),
            pltpu.VMEM((WIDTH, WIDTH), BF16),
            pltpu.VMEM((RING, PIECE, OUT), BF16),
            pltpu.VMEM((TEAM, SLAB, OUT), BF16),
            pltpu.VMEM((4, 3, SLAB, WIDTH), BF16),
            pltpu.VMEM((4, 4, SLAB, WIDTH), BF16),
            pltpu.VMEM((TOKENS, WIDTH), BF16),
            pltpu.VMEM((TOKENS, WIDTH), BF16),
            pltpu.VMEM((TOKENS, 3 * WIDTH), BF16),
            pltpu.VMEM((WINDOWS, HEADS, WINDOW, WINDOW), BF16),
            pltpu.VMEM((TOKENS, WIDTH), BF16),
            pltpu.VMEM((4, CELLS, WIDTH), F32),
            pltpu.VMEM((TEAM, SLAB, WIDTH), BF16),
            pltpu.VMEM((TEAM, SLAB, WIDTH), BF16),
            pltpu.VMEM((TEAM, SLAB, WIDTH), BF16),
            pltpu.VMEM((TEAM, SLAB, WIDTH), BF16),
            pltpu.VMEM((TEAM, SLAB, OUT), BF16),
            pltpu.VMEM((TEAM, SLAB, OUT), BF16),
            pltpu.VMEM((TOKENS, WIDTH), BF16),
            pltpu.VMEM((TOKENS, 3 * WIDTH), BF16),
            pltpu.VMEM((WINDOW * HEADS, LANES), F32),
            pltpu.VMEM((WINDOW * HEADS, LANES), F32),
            pltpu.VMEM((TEAM, HEADS, BUCKETS), F32),
            pltpu.VMEM((RING, HEADS, BUCKETS), F32),
            pltpu.VMEM((BANDS, HEADS, BUCKETS), F32),
            pltpu.VMEM((HEADS, 8, LANES), F32),
            pltpu.VMEM((WINDOW, 2 * LANES), jnp.int32),
            pltpu.VMEM((HEADS, WINDOW, WINDOW), F32),
            pltpu.VMEM((WINDOW, 2 * LANES), jnp.int32),
            pltpu.VMEM((WINDOW, WINDOW, SPLIT), BF16),
            pltpu.SemaphoreType.DMA((3,)),
            pltpu.SemaphoreType.DMA((COPIES,)),
            pltpu.SemaphoreType.DMA((COPIES,)),
        ],
        compiler_params=pltpu.CompilerParams(
            collective_id=0, has_side_effects=True, vmem_limit_bytes=60 * 2**20
        ),
        name="fused_block",
    )(*consts, x, table, index, cot, piece, wqkv, wproj)


def shards(latents, qkv_weight, proj_weight, merge_weight, bias_table, bias_index, cotangent):
    cot = cotangent.transpose(1, 2, 0, 3)
    cells = latents.transpose(1, 2, 0, 3)
    merged, grad, grad_table = fused(
        cells.reshape(-1, 4, WIDTH), bias_table, bias_index, cot.reshape(-1, 4, OUT), merge_weight, qkv_weight, proj_weight
    )
    return (
        merged.reshape(cot.shape).transpose(2, 0, 1, 3),
        grad.reshape(cells.shape).transpose(2, 0, 1, 3),
        grad_table,
    )


def solution(mesh):
    return jax.shard_map(
        shards,
        mesh=mesh,
        in_specs=(
            P(None, "lat", "lon", None),
            P(),
            P(),
            P("lon", None),
            P(),
            P(),
            P(None, "lat", "lon", None),
        ),
        out_specs=(P(None, "lat", "lon", None), P(None, "lat", "lon", None), P()),
        check_vma=False,
    )
```

```python
import jax
import jax.numpy as jnp
import numpy as np
from jax import lax
from jax.experimental import pallas as pl
from jax.experimental.pallas import tpu as pltpu
from jax.sharding import PartitionSpec as P

EPS = 1e-05
MASKED = -1e30
HEADS = 16
PAIRS = 8
HEAD_DIM = 64
WINDOW = 144
WINDOWS = 2
TOKENS = WINDOW * WINDOWS
WIDTH = 1024
OUT = 2048
BUCKETS = 768
LANES = 128
SPLIT = 256
TEAM = 4
RING = 8
BANDS = 8
PIECE = 128
CELLS = 72
SLAB = 80
F32 = jnp.float32
BF16 = jnp.bfloat16
LAST = (((1,), (1,)), ((), ()))
FIRST = (((0,), (0,)), ((), ()))
MESH = pl.DeviceIdType.MESH


def dot(a, b, dims=(((1,), (0,)), ((), ()))):
    return lax.dot_general(a, b, dims, preferred_element_type=F32)


def lanes(start, size=LANES):
    return pl.ds(pl.multiple_of(start, LANES), size)


def quad_row(level, row, col):
    quad = 2 * (row // 6) + col // 3
    return quad * CELLS + level * 18 + (row % 6) * 3 + col % 3


def orders():
    natural = np.zeros((TOKENS, TOKENS), np.float32)
    window = np.zeros((TOKENS, TOKENS), np.float32)
    merge = np.zeros((TOKENS, TOKENS), np.float32)
    for level in range(4):
        for row in range(12):
            for col in range(6):
                cell = (level * 12 + row) * 6 + col
                place = quad_row(level, row, col)
                natural[place, (row * 6 + col) * 4 + level] = 1
                source = quad_row((level + 1) % 4, (row + 6) % 12, (col + 3) % 6)
                window[cell, source] = 1
                spot = 2 * (col % 2) + row % 2
                merge[spot * CELLS + (row // 2 * 3 + col // 2) * 4 + level, place] = 1
    return [jnp.asarray(m, BF16) for m in (natural, window, window.T, merge, merge.T, natural.T)]


def stats(values):
    average = jnp.mean(values, axis=-1, keepdims=True)
    centered = values - average
    variance = jnp.mean(centered * centered, axis=-1, keepdims=True)
    return centered, lax.rsqrt(variance + EPS)


def half_mask(shape, half):
    lane = lax.broadcasted_iota(jnp.int32, shape, 1)
    return (lane >= HEAD_DIM) if half else (lane < HEAD_DIM)


def region_code(shape, axis, window, is_last):
    token = lax.broadcasted_iota(jnp.int32, shape, axis)
    level = (token >= 72).astype(jnp.int32)
    row = token - 72 * level
    late = (row >= 36).astype(jnp.int32)
    return late * is_last + (2 * level if window == 1 else 0)


def allowed_pairs(window, is_last):
    shape = (WINDOW, WINDOW)
    return region_code(shape, 0, window, is_last) == region_code(shape, 1, window, is_last)


def gather_bias(table_ref, index_ref, head):
    tiles = []
    for tile in range(2):
        index = index_ref[:, tile * LANES:(tile + 1) * LANES]
        low = index & (LANES - 1)
        high = index >> 7
        found = None
        for chunk in range(BUCKETS // LANES):
            row = table_ref[head, chunk:chunk + 1, :]
            spread = jnp.broadcast_to(row, (WINDOW, LANES))
            part = jnp.take_along_axis(spread, low, axis=1, mode="promise_in_bounds")
            found = part if found is None else jnp.where(high == chunk, part, found)
        tiles.append(found)
    return jnp.concatenate(tiles, axis=1)[:, :WINDOW]


def attend_pair(pair, is_last, biases, packed, probs_ref, attended):
    base = pair * LANES
    bias = [biases[2 * pair + half] for half in range(2)]
    masks = [half_mask((WINDOW, LANES), half) for half in range(2)]
    zero = jnp.zeros((WINDOW, LANES), BF16)
    for window in range(WINDOWS):
        rows = slice(window * WINDOW, (window + 1) * WINDOW)
        allowed = allowed_pairs(window, is_last)
        query = packed[rows, lanes(base)] * jnp.array(HEAD_DIM ** -0.5, BF16)
        key = packed[rows, lanes(WIDTH + base)]
        value = packed[rows, lanes(2 * WIDTH + base)]
        mixed = None
        for half in range(2):
            scores = dot(jnp.where(masks[half], query, zero), key, LAST)
            scores = jnp.where(allowed, scores + bias[half], MASKED)
            weights = jnp.exp(scores - jnp.max(scores, axis=-1, keepdims=True))
            probs = (weights * (1.0 / jnp.sum(weights, axis=-1, keepdims=True))).astype(BF16)
            probs_ref[window, 2 * pair + half] = probs
            term = dot(probs, jnp.where(masks[half], value, zero))
            mixed = term if mixed is None else mixed + term
        attended[rows, lanes(base)] = mixed.astype(BF16)


def unattend_pair(pair, packed, probs_ref, datt, dpacked, dmain, dtail):
    base = pair * LANES
    scale = jnp.array(HEAD_DIM ** -0.5, BF16)
    masks = [half_mask((WINDOW, LANES), half) for half in range(2)]
    zero = jnp.zeros((WINDOW, LANES), BF16)
    sums = [None, None]
    for window in range(WINDOWS):
        rows = slice(window * WINDOW, (window + 1) * WINDOW)
        query = packed[rows, lanes(base)] * scale
        key = packed[rows, lanes(WIDTH + base)] * scale
        value = packed[rows, lanes(2 * WIDTH + base)]
        out_grad = datt[rows, lanes(base)]
        dquery, dkey, dvalue = None, None, None
        for half in range(2):
            grad = jnp.where(masks[half], out_grad, zero)
            probs = probs_ref[window, 2 * pair + half]
            wide = probs.astype(F32)
            product = wide * dot(grad, value, LAST)
            ds = product - wide * jnp.sum(product, axis=-1, keepdims=True)
            sums[half] = ds if sums[half] is None else sums[half] + ds
            narrow = ds.astype(BF16)
            one = dot(narrow, jnp.where(masks[half], key, zero))
            two = dot(narrow, jnp.where(masks[half], query, zero), FIRST)
            three = dot(probs, grad, FIRST)
            dquery = one if dquery is None else dquery + one
            dkey = two if dkey is None else dkey + two
            dvalue = three if dvalue is None else dvalue + three
        dpacked[rows, lanes(base)] = dquery.astype(BF16)
        dpacked[rows, lanes(WIDTH + base)] = dkey.astype(BF16)
        dpacked[rows, lanes(2 * WIDTH + base)] = dvalue.astype(BF16)
    for half in range(2):
        total = jnp.concatenate([sums[half], jnp.zeros((WINDOW, 2 * LANES - WINDOW), F32)], axis=1)
        for tile, store in enumerate((dmain, dtail)):
            cols = slice(tile * LANES, (tile + 1) * LANES)
            store[pl.ds(2 * pair + half, WINDOW, stride=HEADS), :] = total[:, cols]


def build_hots(index_ref, lows, hots):
    shape = (WINDOW, WINDOW)
    eye = lax.broadcasted_iota(jnp.int32, shape, 0) == lax.broadcasted_iota(jnp.int32, shape, 1)
    eye = jnp.where(eye, 1.0, 0.0).astype(BF16)
    low = (index_ref[:, :WINDOW] & (SPLIT - 1)).astype(F32).astype(BF16)
    flipped = dot(eye, low, LAST).astype(jnp.int32)
    lows[...] = jnp.concatenate([flipped, jnp.zeros((WINDOW, 2 * LANES - WINDOW), jnp.int32)], axis=1)
    bucket = lax.broadcasted_iota(jnp.int32, (WINDOW, SPLIT), 1)

    def build(tile):
        def step(row, carry):
            wanted = jnp.zeros((WINDOW, LANES), jnp.int32) + (row - tile * LANES)
            source = lows[:, tile * LANES:(tile + 1) * LANES]
            spread = jnp.take_along_axis(source, wanted, axis=1, mode="promise_in_bounds")
            spread = jnp.concatenate([spread, spread], axis=1)
            hots[row] = jnp.where(bucket == spread, 1.0, 0.0).astype(BF16)
            return carry

        return step

    lax.fori_loop(0, LANES, build(0), 0, unroll=4)
    lax.fori_loop(LANES, WINDOW, build(1), 0, unroll=4)


def scatter_table(index_ref, hots, dmain, dtail):
    def scatter_row(row, total):
        here = pl.ds(pl.multiple_of(row * HEADS, HEADS), HEADS)
        block = jnp.concatenate([dmain[here, :], dtail[here, :]], axis=1)[:, :WINDOW]
        high = index_ref[pl.ds(row, 1), :][:, :WINDOW] >> 8
        parts = jnp.concatenate(
            [jnp.where(high == part, block, 0.0) for part in range(BUCKETS // SPLIT)], axis=0
        )
        coarse = parts.astype(BF16)
        fine = (parts - coarse.astype(F32)).astype(BF16)
        return total + dot(jnp.concatenate([coarse, fine], axis=0), hots[row])

    rows = HEADS * (BUCKETS // SPLIT)
    total = lax.fori_loop(0, WINDOW, scatter_row, jnp.zeros((2 * rows, SPLIT), F32), unroll=8)
    total = total[:rows] + total[rows:]
    return jnp.concatenate([total[part * HEADS:(part + 1) * HEADS] for part in range(BUCKETS // SPLIT)], axis=1)


def pad_rows(values):
    return jnp.concatenate([values, jnp.zeros((SLAB - CELLS, values.shape[1]), F32)], axis=0).astype(BF16)


def kernel(
    nat2quad, quad2win, win2quad, quad2merge, merge2quad, quad2nat,
    x_ref, table_ref, raw_index, cot_ref, piece_hbm, wqkv_hbm, wproj_hbm,
    merged_ref, grad_ref, bias_ref,
    wqkv, wproj, wbuf, cots, sent, landed, tokens, normed, packed, probs, attended,
    hats, gsend, grecv, msend, mrecv, psend, precv, datt, dpacked, dmain, dtail,
    sum_team, sum_ring, sum_bands, chunks, index_ref, biases, lows, hots, local_sems, send_sems, recv_sems,
):
    lon = lax.axis_index("lon")
    lat = lax.axis_index("lat")
    ring = lon // TEAM
    member = lax.rem(lon, TEAM)
    lons = RING * TEAM
    is_last = (lat == BANDS - 1).astype(jnp.int32)

    def team_peer(step):
        return {"lon": ring * TEAM + lax.rem(member + step, TEAM), "lat": lat}

    def ring_peer(step):
        return {"lon": lax.rem(ring + step, RING) * TEAM + member, "lat": lat}

    def band_peer(step):
        return {"lon": lon, "lat": lax.rem(lat + step, BANDS)}

    def near(rows, cols):
        return {"lon": lax.rem(lon + cols + lons, lons), "lat": lax.rem(lat + rows + BANDS, BANDS)}

    peers = [team_peer(step) for step in range(1, TEAM)]
    peers += [ring_peer(step) for step in range(1, RING)]
    peers += [band_peer(step) for step in range(1, BANDS)]
    peers += [near(0, 1), near(0, -1), near(1, 1), near(-1, -1)]

    loads = [
        pltpu.make_async_copy(wqkv_hbm, wqkv, local_sems.at[0]),
        pltpu.make_async_copy(wproj_hbm, wproj, local_sems.at[1]),
        pltpu.make_async_copy(piece_hbm, wbuf.at[ring], local_sems.at[2]),
    ]
    for load in loads:
        load.start()

    barrier = pltpu.get_barrier_semaphore()
    for peer in peers:
        pl.semaphore_signal(barrier, inc=1, device_id=peer, device_id_type=MESH)

    copies = []

    def remote(source, target, peer):
        slot = len(copies)
        copy = pltpu.make_async_remote_copy(
            src_ref=source, dst_ref=target, send_sem=send_sems.at[slot], recv_sem=recv_sems.at[slot],
            device_id=peer, device_id_type=MESH,
        )
        copies.append(copy)
        return copy

    def exchange(stage, side):
        moves = []
        for quad, (rows, cols) in enumerate(((1, 1), (1, 0), (0, 1))):
            moves.append(remote(sent.at[stage, quad], landed.at[stage, quad], near(side * rows, side * cols)))
        return moves

    def fill(stage, order, values):
        rows = dot(order[...], values)
        for quad in range(4):
            part = rows[quad * CELLS:(quad + 1) * CELLS]
            part = jnp.concatenate([part[:, :WIDTH // 2], part[:, WIDTH // 2:]], axis=0).astype(BF16)
            if quad == 3:
                landed[stage, quad] = part
            else:
                sent[stage, quad] = part

    def arrived(stage, order):
        block = landed[stage].astype(F32)
        rows = jnp.concatenate([block[:, :CELLS], block[:, CELLS:]], axis=2)
        return dot(order[...], rows.reshape(TOKENS, WIDTH).astype(BF16))

    index_ref[...] = jnp.concatenate(
        [raw_index[...], jnp.zeros((WINDOW, 2 * LANES - WINDOW), jnp.int32)], axis=1
    )
    fill(0, nat2quad, x_ref[...].astype(F32).reshape(TOKENS, WIDTH).astype(BF16))
    cots[member] = pad_rows(cot_ref[...].astype(F32).reshape(CELLS, OUT))
    pl.semaphore_wait(barrier, len(peers))

    first = exchange(0, -1)
    for copy in first:
        copy.start()

    side = lax.rem(lat // 2, 2)
    quarter = PIECE // 4

    def share(part, count=1):
        return pl.ds(pl.multiple_of(side * (2 * quarter) + part * quarter, quarter), count * quarter)

    def above(step):
        return lax.rem(ring - step + RING, RING)

    def below(step):
        return lax.rem(ring + step, RING)

    ahead, behind, across = [], [], [[]]
    for step in range(4):
        if step == 0:
            ahead.append(remote(piece_hbm.at[share(0, 2)], wbuf.at[ring, share(0, 2)], ring_peer(1)))
            behind.append(remote(piece_hbm.at[share(0, 2)], wbuf.at[ring, share(0, 2)], ring_peer(RING - 1)))
        else:
            up = wbuf.at[above(step), share(0, 2 if step < 3 else 1)]
            down = wbuf.at[below(step), share(0, 2) if step < 3 else share(1)]
            ahead.append(remote(up, up, ring_peer(1)))
            behind.append(remote(down, down, ring_peer(RING - 1)))
    for step in range(1, 5):
        moves = []
        for spot in (above(step), below(step)) if step < 4 else (below(step),):
            for part, peer in ((0, band_peer(2)), (1, band_peer(BANDS - 2))):
                moves.append(remote(wbuf.at[spot, share(part)], wbuf.at[spot, share(part)], peer))
        across.append(moves)

    def ring_step(step):
        if step > 0:
            ahead[step - 1].wait_recv()
            behind[step - 1].wait_recv()
        if step < 4:
            ahead[step].start()
            behind[step].start()
        for copy in across[step]:
            copy.start()

    def across_wait(step):
        for copy in across[step]:
            copy.wait_recv()

    spread = [remote(cots.at[member], cots.at[member], team_peer(step)) for step in range(1, TEAM)]
    ring_step(0)

    for chunk in range(BUCKETS // LANES):
        cols = table_ref[:, chunk * LANES:min((chunk + 1) * LANES, table_ref.shape[1])]
        if cols.shape[1] < LANES:
            cols = jnp.concatenate([cols, jnp.zeros((HEADS, LANES - cols.shape[1]), F32)], axis=1)
        for head in range(HEADS):
            chunks[head, chunk:chunk + 1, :] = cols[head:head + 1, :]

    def bias_step(head, carry):
        biases[head] = gather_bias(chunks, index_ref, head)
        return carry

    lax.fori_loop(0, HEADS, bias_step, 0, unroll=4)

    for copy in first:
        copy.wait_recv()
    for copy in spread:
        copy.start()
    ring_step(1)
    values = arrived(0, quad2win)
    tokens[...] = values.astype(BF16)
    centered, inverse = stats(values)
    normed[...] = (centered * inverse).astype(BF16)
    loads[0].wait()
    for part in range(12):
        cols = slice(part * 256, (part + 1) * 256)
        packed[:, cols] = dot(normed[...], wqkv[:, cols]).astype(BF16)

    def attend_step(pair, carry):
        attend_pair(pair, is_last, biases, packed, probs, attended)
        return carry

    lax.fori_loop(0, PAIRS // 2, attend_step, 0, unroll=PAIRS // 2)
    ring_step(2)
    lax.fori_loop(PAIRS // 2, PAIRS, attend_step, 0, unroll=PAIRS // 2)
    loads[1].wait()
    block = tokens[...].astype(F32) + dot(attended[...], wproj[...])
    fill(1, win2quad, block.astype(BF16))
    second = exchange(1, 1)
    for copy in second:
        copy.start()

    for copy in spread:
        copy.wait_recv()
    loads[2].wait()

    def merge_grad(spot):
        rows = dot(cots[...].reshape(TEAM * SLAB, OUT), wbuf[spot], LAST).astype(BF16)
        here = pl.ds(pl.multiple_of(spot * PIECE, PIECE), PIECE)
        gsend[:, :, here] = rows.reshape(TEAM, SLAB, PIECE)

    def merge_both(step):
        merge_grad(above(step))
        merge_grad(below(step))

    merge_grad(ring)
    ring_step(3)
    across_wait(1)
    merge_both(1)
    across_wait(2)
    merge_both(2)
    ring_step(4)

    for copy in second:
        copy.wait_recv()
    slabs = arrived(1, quad2merge)
    parts = [slabs[spot * CELLS:(spot + 1) * CELLS] for spot in range(4)]
    total = sum(jnp.sum(part, axis=-1, keepdims=True) for part in parts)
    average = total * (1.0 / (4 * WIDTH))
    parts = [part - average for part in parts]
    total = sum(jnp.sum(part * part, axis=-1, keepdims=True) for part in parts)
    merge_inverse = lax.rsqrt(total * (1.0 / (4 * WIDTH)) + EPS)
    for spot in range(4):
        hat = parts[spot] * merge_inverse
        hats[spot] = hat
        rows = pad_rows(hat)
        for block_id in range(8):
            target = (2 * spot + block_id // 4) * PIECE
            msend[block_id % 4, :, target:target + PIECE] = rows[:, block_id * PIECE:(block_id + 1) * PIECE]
    mrecv[member] = msend[member]
    inputs = [
        remote(msend.at[lax.rem(member + step, TEAM)], mrecv.at[member], team_peer(step))
        for step in range(1, TEAM)
    ]
    for copy in inputs:
        copy.start()

    across_wait(3)
    merge_both(3)
    across_wait(4)
    merge_grad(below(4))
    grecv[member] = gsend[member]
    grads = [
        remote(gsend.at[lax.rem(member + step, TEAM)], grecv.at[member], team_peer(step))
        for step in range(1, TEAM)
    ]
    for copy in grads:
        copy.start()

    for copy in inputs:
        copy.wait_recv()
    for part in range(8):
        cols = slice(part * 256, (part + 1) * 256)
        rows = dot(mrecv[...].reshape(TEAM * SLAB, WIDTH), wbuf[:, :, cols].reshape(RING * PIECE, 256))
        psend[:, :, cols] = rows.astype(BF16).reshape(TEAM, SLAB, 256)
    precv[member] = psend[member]
    partials = [
        remote(psend.at[lax.rem(member + step, TEAM)], precv.at[member], team_peer(step))
        for step in range(1, TEAM)
    ]
    for copy in grads:
        copy.wait_recv()
    slopes = []
    for spot in range(4):
        blocks = [
            grecv[block_id % 4, :, (2 * spot + block_id // 4) * PIECE:(2 * spot + block_id // 4 + 1) * PIECE]
            for block_id in range(8)
        ]
        slopes.append(jnp.concatenate(blocks, axis=1).astype(F32)[:CELLS])
    mean_slope = sum(jnp.sum(s, axis=-1, keepdims=True) for s in slopes) * (1.0 / (4 * WIDTH))
    mean_tilt = sum(
        jnp.sum(s * hats[spot], axis=-1, keepdims=True) for spot, s in enumerate(slopes)
    ) * (1.0 / (4 * WIDTH))
    slopes = [merge_inverse * (s - mean_slope - hats[spot] * mean_tilt) for spot, s in enumerate(slopes)]
    fill(2, merge2quad, jnp.concatenate(slopes, axis=0).astype(BF16))
    third = exchange(2, -1)
    for copy in third:
        copy.start()
    build_hots(index_ref, lows, hots)
    for copy in third:
        copy.wait_recv()
    for copy in partials:
        copy.start()
    attended[...] = arrived(2, quad2win).astype(BF16)
    datt[...] = dot(attended[...], wproj[...], LAST).astype(BF16)

    def unattend_step(pair, carry):
        unattend_pair(pair, packed, probs, datt, dpacked, dmain, dtail)
        return carry

    lax.fori_loop(0, PAIRS, unattend_step, 0, unroll=PAIRS)
    sum_team[member] = scatter_table(index_ref, hots, dmain, dtail)
    team_sums = [remote(sum_team.at[member], sum_team.at[member], team_peer(step)) for step in range(1, TEAM)]
    for copy in team_sums:
        copy.start()

    dnormed = dot(dpacked[...], wqkv[...], LAST).astype(BF16).astype(F32)
    centered, inverse = stats(tokens[...].astype(F32))
    hat = centered * inverse
    slope = jnp.mean(dnormed * hat, axis=-1, keepdims=True)
    inner = inverse * (dnormed - jnp.mean(dnormed, axis=-1, keepdims=True) - hat * slope)
    fill(3, win2quad, (attended[...].astype(F32) + inner).astype(BF16))
    fourth = exchange(3, 1)
    for copy in fourth:
        copy.start()

    for copy in team_sums:
        copy.wait_recv()
    sum_ring[ring] = sum_team[0] + sum_team[1] + sum_team[2] + sum_team[3]
    ring_sums = [remote(sum_ring.at[ring], sum_ring.at[ring], ring_peer(step)) for step in range(1, RING)]
    for copy in ring_sums:
        copy.start()

    for copy in partials:
        copy.wait_recv()
    for part in range(8):
        cols = slice(part * 256, (part + 1) * 256)
        total = precv[0, :, cols].astype(F32)
        for peer in range(1, TEAM):
            total = total + precv[peer, :, cols].astype(F32)
        merged_ref[:, :, cols] = total[:CELLS].reshape(-1, 4, 256).astype(BF16)

    for copy in ring_sums:
        copy.wait_recv()
    total = sum_ring[0]
    for peer in range(1, RING):
        total = total + sum_ring[peer]
    sum_bands[lat] = total
    band_sums = [remote(sum_bands.at[lat], sum_bands.at[lat], band_peer(step)) for step in range(1, BANDS)]
    for copy in band_sums:
        copy.start()

    for copy in fourth:
        copy.wait_recv()
    grad_ref[...] = arrived(3, quad2nat).reshape(-1, 4, WIDTH).astype(BF16)

    for copy in band_sums:
        copy.wait_recv()
    total = sum_bands[0]
    for peer in range(1, BANDS):
        total = total + sum_bands[peer]
    bias_ref[...] = total[:, :bias_ref.shape[1]]
    for copy in copies:
        copy.wait_send()


COPIES = 12 + 8 + 14 + 4 * 3 + 3 + 7 + 7


def fused(x, table, index, cot, piece, wqkv, wproj):
    consts = orders()
    vmem = pl.BlockSpec(memory_space=pltpu.VMEM)
    anywhere = pl.BlockSpec(memory_space=pl.ANY)
    return pl.pallas_call(
        kernel,
        out_shape=(
            jax.ShapeDtypeStruct(cot.shape, BF16),
            jax.ShapeDtypeStruct(x.shape, BF16),
            jax.ShapeDtypeStruct(table.shape, F32),
        ),
        in_specs=[vmem] * 10 + [anywhere] * 3,
        out_specs=[vmem] * 3,
        scratch_shapes=[
            pltpu.VMEM((WIDTH, 3 * WIDTH), BF16),
            pltpu.VMEM((WIDTH, WIDTH), BF16),
            pltpu.VMEM((RING, PIECE, OUT), BF16),
            pltpu.VMEM((TEAM, SLAB, OUT), BF16),
            pltpu.VMEM((4, 3, 2 * CELLS, WIDTH // 2), BF16),
            pltpu.VMEM((4, 4, 2 * CELLS, WIDTH // 2), BF16),
            pltpu.VMEM((TOKENS, WIDTH), BF16),
            pltpu.VMEM((TOKENS, WIDTH), BF16),
            pltpu.VMEM((TOKENS, 3 * WIDTH), BF16),
            pltpu.VMEM((WINDOWS, HEADS, WINDOW, WINDOW), BF16),
            pltpu.VMEM((TOKENS, WIDTH), BF16),
            pltpu.VMEM((4, CELLS, WIDTH), F32),
            pltpu.VMEM((TEAM, SLAB, WIDTH), BF16),
            pltpu.VMEM((TEAM, SLAB, WIDTH), BF16),
            pltpu.VMEM((TEAM, SLAB, WIDTH), BF16),
            pltpu.VMEM((TEAM, SLAB, WIDTH), BF16),
            pltpu.VMEM((TEAM, SLAB, OUT), BF16),
            pltpu.VMEM((TEAM, SLAB, OUT), BF16),
            pltpu.VMEM((TOKENS, WIDTH), BF16),
            pltpu.VMEM((TOKENS, 3 * WIDTH), BF16),
            pltpu.VMEM((WINDOW * HEADS, LANES), F32),
            pltpu.VMEM((WINDOW * HEADS, LANES), F32),
            pltpu.VMEM((TEAM, HEADS, BUCKETS), F32),
            pltpu.VMEM((RING, HEADS, BUCKETS), F32),
            pltpu.VMEM((BANDS, HEADS, BUCKETS), F32),
            pltpu.VMEM((HEADS, 8, LANES), F32),
            pltpu.VMEM((WINDOW, 2 * LANES), jnp.int32),
            pltpu.VMEM((HEADS, WINDOW, WINDOW), F32),
            pltpu.VMEM((WINDOW, 2 * LANES), jnp.int32),
            pltpu.VMEM((WINDOW, WINDOW, SPLIT), BF16),
            pltpu.SemaphoreType.DMA((3,)),
            pltpu.SemaphoreType.DMA((COPIES,)),
            pltpu.SemaphoreType.DMA((COPIES,)),
        ],
        compiler_params=pltpu.CompilerParams(
            collective_id=0, has_side_effects=True, vmem_limit_bytes=60 * 2**20
        ),
        name="fused_block",
    )(*consts, x, table, index, cot, piece, wqkv, wproj)


def shards(latents, qkv_weight, proj_weight, merge_weight, bias_table, bias_index, cotangent):
    cot = cotangent.transpose(1, 2, 0, 3)
    cells = latents.transpose(1, 2, 0, 3)
    merged, grad, grad_table = fused(
        cells.reshape(-1, 4, WIDTH), bias_table, bias_index, cot.reshape(-1, 4, OUT), merge_weight, qkv_weight, proj_weight
    )
    return (
        merged.reshape(cot.shape).transpose(2, 0, 1, 3),
        grad.reshape(cells.shape).transpose(2, 0, 1, 3),
        grad_table,
    )


def solution(mesh):
    return jax.shard_map(
        shards,
        mesh=mesh,
        in_specs=(
            P(None, "lat", "lon", None),
            P(),
            P(),
            P("lon", None),
            P(),
            P(),
            P(None, "lat", "lon", None),
        ),
        out_specs=(P(None, "lat", "lon", None), P(None, "lat", "lon", None), P()),
        check_vma=False,
    )
```
